512 devices in a mesh: gz: 32 (over x, y), xy: 16 (over z, core).
Axes of the slice: x: 4, y: 8, z: 8, core: 2. Of those that a mesh axis runs over, the one named last changes fastest.
Arguments:
- features: bfloat16 [64, 128, 64, 128], P(None, 'gz', 'xy'), may hold values from -6 to 6
- conv_w: bfloat16 [64, 64, 3, 3, 3], replicated, may hold values from -0.15625 to 0.15625
- conv_b: float32 [64], replicated, may hold values from -4 to 4
- head_w: bfloat16 [3, 64], replicated, may hold values from -1.796875 to 1.796875
- head_b: float32 [3], replicated, may hold values from -3 to 3
- bins: int32 [128, 64, 128], P('gz', 'xy'), may hold values from 0 to 15
- edge_ids: int32 [3, 128, 64, 128], P(None, 'gz', 'xy'), may hold values from -1 to 4095, as said below
- owner_map: int32 [4096], replicated, may hold values from 0 to 4095, each once
Outputs:
- blended: float32 [3, 128, 64, 128], P(None, 'gz', 'xy')
- edge_hist: float32 [512, 128], P(('gz', 'xy'))
The draws below stay inside these ranges and needn't reach their ends.
Inputs may be any that keep to these rules, and one draw needn't show every extreme that they name: `edge_ids`: -1 marks a face without contact, among them every face on the volume's last plane along its own axis; every other value is an edge id, 4095 among them.
All inputs are finite; a program needn't handle non-finite values.
Results may differ from the reference program's by a relative error of at most 0.0024.
Values may be sent and summed in bfloat16 or wider, within the bound.
No kernel may reach another device: no remote copies, remote signals or barrier semaphores. Data moves between devices by JAX's collectives and lax.ppermute only.
A program may use at most 64 MiB of HBM per device.

```python
import jax
import jax.numpy as jnp
from jax import lax

CH = 64
AFF = 3
BINS = 16
MARGIN = 2
CZ = 4
CY = 4
E_OWN = 8
Z = 128
Y = 64
X = 128
OWNERS = 512
EDGES = 4096
N_GZ = 32
N_XY = 16


def draw_edge_ids(key, part):
    key = jax.random.fold_in(key, 7)
    first, second = jax.random.split(key)
    shape = (AFF, Z, Y, X)
    ids = jax.random.randint(first, shape, 0, EDGES)
    live = jax.random.randint(second, shape, 0, 5) < 3
    zcell = jnp.arange(Z)[:, None, None] == Z - 1
    ycell = jnp.arange(Y)[None, :, None] == Y - 1
    xcell = jnp.arange(X)[None, None, :] == X - 1
    last = jnp.stack([jnp.broadcast_to(zcell, (Z, Y, X)), jnp.broadcast_to(ycell, (Z, Y, X)), jnp.broadcast_to(xcell, (Z, Y, X))])
    ids = jnp.where(live & jnp.logical_not(last), ids, -1)
    ids = ids.at[0, 0, 0, 0].set(EDGES - 1)
    return ids.astype(jnp.int32)


def place_ends(values, key, low, high):
    index_at = [jax.random.randint(jax.random.fold_in(key, axis), (), 0, length) for axis, length in enumerate(values.shape)]
    longest = values.shape.index(max(values.shape))
    beside = index_at[:longest] + [(index_at[longest] + 1) % values.shape[longest]] + index_at[longest + 1:]
    return values.at[tuple(index_at)].set(low).at[tuple(beside)].set(high)


def steps_of(stream_key, shape, shards, least, largest):
    def one(axis_at, parts):
        heights = jax.random.uniform(jax.random.fold_in(jax.random.fold_in(stream_key, 6), axis_at), (parts,), jnp.float32, least / len(shards), largest / len(shards))
        return jnp.repeat(jnp.exp(heights), shape[axis_at] // parts).reshape((-1,) + (1,) * (len(shape) - axis_at - 1))

    gain = one(*shards[0])
    for cut in shards[1:]:
        gain = gain * one(*cut)
    return gain


def noise(stream_key, dims, spread, reach, cuts=(), held_as=jnp.bfloat16):
    drawn = jax.random.normal(stream_key, dims, jnp.float32) * spread
    if len(cuts) > 0:
        drawn = steps_of(stream_key, dims, cuts, -0.22, 0.18) * drawn
    return jnp.clip(drawn, min=-reach, max=reach).astype(held_as)


def setup_inputs(seed: int = 0) -> dict:
    arg_keys = jax.random.split(jax.random.key(seed), 9)
    features = noise(arg_keys[0], (CH, Z, Y, X), 1.0, 6.0, ((1, 32), (2, 16)))
    conv_w = noise(arg_keys[1], (CH, CH, 3, 3, 3), (27 * CH) ** -0.5, 0.15625)
    conv_b = noise(arg_keys[2], (CH,), 1.0, 4.0, (), jnp.float32)
    head_w = noise(arg_keys[3], (AFF, CH), 0.3, 1.796875)
    head_b = noise(arg_keys[4], (AFF,), 1.0, 3.0, (), jnp.float32)
    bins = place_ends(jax.random.randint(arg_keys[5], (Z, Y, X), 0, BINS), jax.random.fold_in(arg_keys[5], 1), 0, BINS - 1).astype(jnp.int32)
    edge_ids = draw_edge_ids(jax.random.fold_in(arg_keys[8], 71), 0)
    owner_map = jax.random.permutation(arg_keys[7], EDGES).astype(jnp.int32)
    return dict(features=features, conv_w=conv_w, conv_b=conv_b, head_w=head_w, head_b=head_b, bins=bins, edge_ids=edge_ids, owner_map=owner_map)


def bump(extent):
    cells = jnp.arange(extent).astype(jnp.float32)
    return jnp.minimum(cells, extent - 1 - cells) + 1.0


def reference(features, conv_w, conv_b, head_w, head_b, bins, edge_ids, owner_map):
    zext = CZ + 2 * MARGIN
    yext = CY + 2 * MARGIN
    padded = jnp.pad(features, ((0, 0), (MARGIN, MARGIN), (MARGIN, MARGIN), (0, 0)))
    window = bump(zext)[:, None] * bump(yext)[None, :]
    zero = jnp.zeros((), jnp.int32)

    def one_group(carry, index):
        numer, denom = carry
        zpos = (index // N_XY * CZ).astype(jnp.int32)
        ypos = (index % N_XY * CY).astype(jnp.int32)
        ext = lax.dynamic_slice(padded, (zero, zpos, ypos, zero), (CH, zext, yext, X))
        pre = lax.conv_general_dilated(ext[None], conv_w, (1, 1, 1), ((1, 1), (1, 1), (1, 1)),
                                       dimension_numbers=("NCDHW", "OIDHW", "NCDHW"),
                                       preferred_element_type=jnp.float32)[0]
        hidden = jnp.maximum(pre + conv_b[:, None, None, None], 0.0).astype(jnp.bfloat16)
        logits = jnp.einsum("ac,czyx->azyx", head_w.astype(jnp.float32), hidden.astype(jnp.float32),
                            precision=lax.Precision.HIGHEST)
        pred = jax.nn.sigmoid(logits + head_b[:, None, None, None])
        term = pred * window[None, :, :, None]
        start = (zero, zpos, ypos, zero)
        numer = lax.dynamic_update_slice(numer, lax.dynamic_slice(numer, start, term.shape) + term, start)
        dstart = (zpos, ypos)
        denom = lax.dynamic_update_slice(denom, lax.dynamic_slice(denom, dstart, window.shape) + window, dstart)
        return (numer, denom), None

    numer = jnp.zeros((AFF, Z + 2 * MARGIN, Y + 2 * MARGIN, X), jnp.float32)
    denom = jnp.zeros((Z + 2 * MARGIN, Y + 2 * MARGIN), jnp.float32)
    (numer, denom), _ = lax.scan(one_group, (numer, denom), jnp.arange(N_GZ * N_XY).astype(jnp.int32))
    numer = numer[:, MARGIN:MARGIN + Z, MARGIN:MARGIN + Y]
    denom = denom[MARGIN:MARGIN + Z, MARGIN:MARGIN + Y]
    blended = numer / denom[None, :, :, None]
    valid = edge_ids >= 0
    slots = owner_map[jnp.maximum(edge_ids, 0)]
    index = slots * BINS + bins[None]
    values = jnp.where(valid, blended, 0.0)
    table = jax.ops.segment_sum(values.reshape(-1), index.reshape(-1).astype(jnp.int32), num_segments=EDGES * BINS)
    return blended, table.reshape(OWNERS, E_OWN * BINS)
```

```python
import jax
import jax.numpy as jnp
from jax import lax
from jax.experimental import pallas as pl
from jax.experimental.pallas import tpu as pltpu
from jax.sharding import PartitionSpec as P

BINS = 16
CORE = 4
TAPS = 3
VMEM_LIMIT = 48 * 1024 * 1024

VARIANTS = (
    (0, (0, 1, 2)),
    (1, (0, 1, 2)),
    (1, (0, 1)),
    (2, (1, 2)),
    (2, (0, 1, 2)),
    (3, (0, 1, 2)),
)


def neighbours(axis, first, last):
    peers = lax.axis_size(axis)
    up = [(i, i + 1) for i in range(peers - 1)]
    down = [(j, i) for i, j in up]
    return lax.ppermute(last, axis, up), lax.ppermute(first, axis, down)


def variant_weights(index, total):
    lower = jnp.where(index > 0, 1.0, 0.0)
    upper = jnp.where(index < total - 1, 1.0, 0.0)
    weights = (3.0 + 2.0 * lower, 4.0, lower, upper, 4.0, 3.0 + 2.0 * upper)
    cover = (3.0 + 2.0 * lower, 4.0 + lower, 4.0 + upper, 3.0 + 2.0 * upper)
    return weights, cover


def prepare_kernel(peers, ids_ref, bins_ref, map_ref, taps_ref, row_ref, col_ref, w_ref):
    ids = jnp.maximum(ids_ref[...], 0)
    table = map_ref[...]
    halves = jnp.concatenate([table // 64, table % 64], axis=0).astype(jnp.float32).astype(jnp.bfloat16)
    which = lax.broadcasted_iota(jnp.int32, (64, 128), 0)
    for r in range(ids.shape[0]):
        one = ids[r : r + 1]
        high = jnp.where(one // 64 == which, 1.0, 0.0).astype(jnp.bfloat16)
        found = lax.dot_general(halves, high, (((1,), (0,)), ((), ())), preferred_element_type=jnp.float32)
        low = one % 64 == which
        upper = jnp.sum(jnp.where(low, found[:64], 0.0), axis=0, keepdims=True)
        lower = jnp.sum(jnp.where(low, found[64:], 0.0), axis=0, keepdims=True)
        slot = upper.astype(jnp.int32) * 64 + lower.astype(jnp.int32)
        owner = slot // 8
        row_ref[r : r + 1] = owner
        col_ref[r : r + 1] = slot % 8 * BINS + bins_ref[r % 16 : r % 16 + 1]
    for dx in range(TAPS):
        rows = jnp.concatenate([taps_ref[t // 3, t % 3, dx] for t in range(9)], axis=1)
        w_ref[64 * dx : 64 * dx + 64, :576] = rows
        w_ref[64 * dx : 64 * dx + 64, 640:1024] = rows[:, 192:]


def main_kernel(
    f_ref, zlo_ref, zhi_ref, ylo_ref, yhi_ref, w_ref, cb_ref, hw_ref, hb_ref, wz_ref, ids_ref, row_ref, col_ref,
    out_ref, table_ref, g_ref, a_ref, b_ref,
):
    zero = jnp.zeros((64, 128), jnp.bfloat16)

    def cell(z, y):
        if y == 0:
            return ylo_ref[z, 0]
        if y == 5:
            return yhi_ref[z, 0]
        if z == 0:
            return zlo_ref[0, y - 1]
        if z == 5:
            return zhi_ref[0, y - 1]
        return f_ref[z - 1, y - 1]

    for z in range(6):
        for dy in range(TAPS):
            for v, (y, kept) in enumerate(VARIANTS):
                part = cell(z, y + dy) if dy in kept else zero
                g_ref[(z * 3 + dy) * 64 : (z * 3 + dy) * 64 + 64, v * 128 : v * 128 + 128] = part

    lane = lax.broadcasted_iota(jnp.int32, (64, 128), 1)
    bias = cb_ref[...]
    head_b = hb_ref[...]
    head_w = hw_ref[...]
    preds = {}
    for zv, (z, kept) in enumerate(VARIANTS):
        w = w_ref[:, :576] if len(kept) == 3 else (w_ref[:, :384] if kept[0] == 0 else w_ref[:, 640:1024])
        first = (z + kept[0]) * 192
        for pair in range(3):
            g = g_ref[first : first + 192 * len(kept), pair * 256 : pair * 256 + 256]
            p = lax.dot_general(w, g, (((1,), (0,)), ((), ())), preferred_element_type=jnp.float32)
            hidden = []
            for half in range(2):
                q = p[:, half * 128 : half * 128 + 128]
                before = jnp.where(lane == 0, 0.0, pltpu.roll(q[:64], 1, 1))
                after = jnp.where(lane == 127, 0.0, pltpu.roll(q[128:], 127, 1))
                pre = before + q[64:128] + after
                hidden.append(jnp.maximum(pre + bias, 0.0).astype(jnp.bfloat16))
            logits = lax.dot_general(
                head_w, jnp.concatenate(hidden, axis=1), (((1,), (0,)), ((), ())), preferred_element_type=jnp.float32
            )
            for half in range(2):
                preds[zv, pair * 2 + half] = jax.nn.sigmoid(logits[:, half * 128 : half * 128 + 128] + head_b)

    blends = {}
    for z in range(CORE):
        for y in range(CORE):
            total = None
            for zv, (zc, _) in enumerate(VARIANTS):
                for yv, (yc, _) in enumerate(VARIANTS):
                    if (zc, yc) == (z, y):
                        term = preds[zv, yv] * (wz_ref[0, zv] * wz_ref[1, yv])
                        total = term if total is None else total + term
            blends[z * CORE + y] = total / (wz_ref[2, z] * wz_ref[2, 4 + y])
    for a in range(3):
        for zy in range(16):
            out_ref[a * 16 + zy : a * 16 + zy + 1, :] = blends[zy][a : a + 1]

    owner = lax.broadcasted_iota(jnp.int32, (256, 128), 0).astype(jnp.float32).astype(jnp.bfloat16)
    column = owner[:128]
    one = jnp.ones((), jnp.bfloat16)
    none = jnp.zeros((), jnp.bfloat16)
    for r in range(48):
        value = jnp.where(ids_ref[r : r + 1] >= 0, out_ref[r : r + 1], 0.0)
        big = value.astype(jnp.bfloat16)
        small = (value - big.astype(jnp.float32)).astype(jnp.bfloat16)
        row = row_ref[r : r + 1].astype(jnp.float32)
        col = col_ref[r : r + 1].astype(jnp.float32).astype(jnp.bfloat16)
        lanes = slice(r * 128, r * 128 + 128)
        a_ref[:256, lanes] = jnp.where(owner == row.astype(jnp.bfloat16), one, none)
        a_ref[256:, lanes] = jnp.where(owner == (row - 256.0).astype(jnp.bfloat16), one, none)
        here = column == col
        b_ref[:128, lanes] = jnp.where(here, big, none)
        b_ref[128:, lanes] = jnp.where(here, small, none)
    both = lax.dot_general(
        a_ref[...], b_ref[...], (((1,), (1,)), ((), ())), preferred_element_type=jnp.float32
    )
    table_ref[...] = (both[:, :128] + both[:, 128:]).astype(jnp.bfloat16)


def vmem(count):
    return [pl.BlockSpec(memory_space=pltpu.VMEM)] * count


def on_device(features, conv_w, conv_b, head_w, head_b, bins, edge_ids, owner_map):
    gz_peers, xy_peers = lax.axis_size("gz"), lax.axis_size("xy")
    cells = jnp.transpose(features, (1, 2, 0, 3))
    zlo, zhi = neighbours("gz", cells[:1], cells[CORE - 1 :])
    ids = edge_ids.reshape(48, 128)
    rows, cols, weights = pl.pallas_call(
        lambda *refs: prepare_kernel(xy_peers, *refs),
        out_shape=(
            jax.ShapeDtypeStruct((48, 128), jnp.int32),
            jax.ShapeDtypeStruct((48, 128), jnp.int32),
            jax.ShapeDtypeStruct((192, 1024), jnp.bfloat16),
        ),
        in_specs=vmem(4),
        out_specs=tuple(vmem(3)),
        compiler_params=pltpu.CompilerParams(vmem_limit_bytes=VMEM_LIMIT),
        name="prepare",
    )(ids, bins.reshape(16, 128), owner_map.reshape(64, 64).T, jnp.transpose(conv_w, (2, 3, 4, 0, 1)))
    first = jnp.concatenate([zlo[:, :1], cells[:, :1], zhi[:, :1]], axis=0)
    last = jnp.concatenate([zlo[:, CORE - 1 :], cells[:, CORE - 1 :], zhi[:, CORE - 1 :]], axis=0)
    ylo, yhi = neighbours("xy", first, last)
    zweights, zcover = variant_weights(lax.axis_index("gz"), gz_peers)
    yweights, ycover = variant_weights(lax.axis_index("xy"), xy_peers)
    blank = (0.0,) * 2
    scalars = jnp.stack(
        [jnp.stack([jnp.asarray(v, jnp.float32) for v in line]) for line in (zweights + blank, yweights + blank, zcover + ycover)]
    )
    blended, table = pl.pallas_call(
        main_kernel,
        out_shape=(
            jax.ShapeDtypeStruct((48, 128), jnp.float32),
            jax.ShapeDtypeStruct((512, 128), jnp.bfloat16),
        ),
        in_specs=vmem(9) + [pl.BlockSpec(memory_space=pltpu.SMEM)] + vmem(3),
        out_specs=tuple(vmem(2)),
        scratch_shapes=[
            pltpu.VMEM((6 * 192, 768), jnp.bfloat16),
            pltpu.VMEM((512, 48 * 128), jnp.bfloat16),
            pltpu.VMEM((256, 48 * 128), jnp.bfloat16),
        ],
        compiler_params=pltpu.CompilerParams(vmem_limit_bytes=VMEM_LIMIT),
        name="blend_and_count",
    )(
        cells, zlo, zhi, ylo, yhi, weights, conv_b.reshape(64, 1),
        jnp.pad(head_w, ((0, 5), (0, 0))), jnp.pad(head_b, (0, 5)).reshape(8, 1), scalars, ids, rows, cols,
    )
    parts = lax.all_to_all(table.reshape(gz_peers, xy_peers, 128), "gz", 0, 0, tiled=True)
    sums = jnp.sum(parts.astype(jnp.float32), axis=0)
    share = jnp.sum(lax.all_to_all(sums, "xy", 0, 0, tiled=True), axis=0, keepdims=True)
    return blended.reshape(3, CORE, CORE, 128), share


def solution(mesh):
    in_specs = (
        P(None, "gz", "xy", None),
        P(),
        P(),
        P(),
        P(),
        P("gz", "xy", None),
        P(None, "gz", "xy", None),
        P(),
    )
    out_specs = (P(None, "gz", "xy", None), P(("gz", "xy"), None))
    return jax.shard_map(
        on_device, mesh=mesh, in_specs=in_specs, out_specs=out_specs, check_vma=False
    )
```

```python
import jax
import jax.numpy as jnp
from jax import lax
from jax.experimental import pallas as pl
from jax.experimental.pallas import tpu as pltpu
from jax.sharding import PartitionSpec as P

BINS = 16
CORE = 4
TAPS = 3
FULL = (0, 1, 2)
VMEM_LIMIT = 32 * 1024 * 1024

VARIANTS = ((0, FULL), (1, FULL), (1, (0, 1)), (2, (1, 2)), (2, FULL), (3, FULL))
INNER = (1, 2, 3, 4)
OUTER = (0, 5)


def neighbours(axis, first, last):
    peers = lax.axis_size(axis)
    up = [(i, i + 1) for i in range(peers - 1)]
    down = [(j, i) for i, j in up]
    return lax.ppermute(last, axis, up), lax.ppermute(first, axis, down)


def variant_weights(axis):
    index, total = lax.axis_index(axis), lax.axis_size(axis)
    lower = jnp.where(index > 0, 1.0, 0.0)
    upper = jnp.where(index < total - 1, 1.0, 0.0)
    weights = (3.0 + 2.0 * lower, 4.0, lower, upper, 4.0, 3.0 + 2.0 * upper)
    cover = (3.0 + 2.0 * lower, 4.0 + lower, 4.0 + upper, 3.0 + 2.0 * upper)
    return weights, cover


def column_of(row, size):
    length = row.shape[1]
    down = lax.broadcasted_iota(jnp.int32, (size, length), 0)
    along = lax.broadcasted_iota(jnp.int32, (size, length), 1)
    return jnp.broadcast_to(jnp.sum(jnp.where(down == along, row, 0.0), axis=1, keepdims=True), (size, 128))


def arrange_kernel(f_ref, cells_ref, yfirst_ref, ylast_ref, zfirst_ref, zlast_ref, wide, f_v, sem):
    copy = pltpu.make_async_copy(f_ref, f_v, sem)
    copy.start()
    copy.wait()
    wide[...] = f_v[...].astype(jnp.float32)
    for y in range(CORE):
        for z in range(CORE):
            cell = wide[pl.ds(z * CORE + y, 64, stride=16), :].astype(jnp.bfloat16)
            cells_ref[y, z] = cell
            if y == 0:
                yfirst_ref[0, z] = cell
            if y == CORE - 1:
                ylast_ref[0, z] = cell
            if z == 0:
                zfirst_ref[y, 0] = cell
            if z == CORE - 1:
                zlast_ref[y, 0] = cell


def prepare_kernel(
    ids_hbm, bins_hbm, map_hbm, taps_hbm, cb_hbm, hb_hbm, hw_hbm,
    a_ref, col_ref, w_ref, bias_ref, off_ref, hw_ref,
    ids_ref, bins_ref, map_ref, taps_ref, cb_ref, hb_ref, row_ref, sems,
):
    pairs = (
        (ids_hbm, ids_ref), (map_hbm, map_ref), (bins_hbm, bins_ref), (taps_hbm, taps_ref), (cb_hbm, cb_ref),
        (hb_hbm, hb_ref), (hw_hbm, hw_ref),
    )
    copies = [pltpu.make_async_copy(src, dst, sems.at[i]) for i, (src, dst) in enumerate(pairs)]
    for copy in copies:
        copy.start()
    for copy in copies:
        copy.wait()
    one = jnp.ones((), jnp.bfloat16)
    none = jnp.zeros((), jnp.bfloat16)
    bins = bins_ref[...]
    for block in range(6):
        rows = slice(block * 8, block * 8 + 8)
        ids = ids_ref[rows]
        edge = jnp.maximum(ids, 0)
        low = edge & 127
        high = edge >> 7
        slot = jnp.zeros((8, 128), jnp.int32)
        for h in range(32):
            line = jnp.broadcast_to(map_ref[h : h + 1], (8, 128))
            slot = jnp.where(high == h, jnp.take_along_axis(line, low, axis=1, mode="promise_in_bounds"), slot)
        owner = slot >> 3
        first = block % 2 * 8
        column = (owner >> 8) * 128 + (slot & 7) * BINS + bins[first : first + 8]
        col_ref[rows] = jnp.where(ids >= 0, column, -1).astype(jnp.float32)
        row_ref[rows] = (owner & 255).astype(jnp.float32)
    count = lax.broadcasted_iota(jnp.int32, (256, 128), 0).astype(jnp.float32).astype(jnp.bfloat16)
    for r in range(48):
        row = row_ref[r : r + 1].astype(jnp.bfloat16)
        a_ref[:, r * 128 : r * 128 + 128] = jnp.where(count == row, one, none)
    for dx in range(TAPS):
        rows = jnp.concatenate([taps_ref[t % 3, t // 3, dx] for t in range(9)], axis=1)
        w_ref[64 * dx : 64 * dx + 64, :576] = rows
        w_ref[64 * dx : 64 * dx + 64, 640:1024] = rows[:, 192:]
    bias_ref[...] = column_of(cb_ref[...], 64)
    off_ref[...] = column_of(hb_ref[...], 8)


def predictions(zs, cell, w_ref, bias_ref, hw_ref, hb_ref, g_ref):
    width = 128 * len(zs)
    zero = jnp.zeros((64, 128), jnp.bfloat16)
    for y in range(6):
        for dz in range(TAPS):
            for i, v in enumerate(zs):
                z, kept = VARIANTS[v]
                part = cell(y, z + dz) if dz in kept else zero
                g_ref[(y * 3 + dz) * 64 : (y * 3 + dz) * 64 + 64, i * 128 : i * 128 + 128] = part
    lane = lax.broadcasted_iota(jnp.int32, (64, 128), 1)
    bias = bias_ref[...]
    preds = {}

    def matmul(left, right):
        return lax.dot_general(left, right, (((1,), (0,)), ((), ())), preferred_element_type=jnp.float32)

    def finish(yv, start, p):
        hidden = []
        for half in range(2):
            q = p[:, half * 128 : half * 128 + 128]
            before = jnp.where(lane == 0, 0.0, pltpu.roll(q[:64], 1, 1))
            after = jnp.where(lane == 127, 0.0, pltpu.roll(q[128:], 127, 1))
            pre = before + q[64:128] + after
            hidden.append(jnp.maximum(pre + bias, 0.0).astype(jnp.bfloat16))
        logits = matmul(hw_ref[...], jnp.concatenate(hidden, axis=1))
        for half in range(2):
            logit = logits[:, half * 128 : half * 128 + 128] + hb_ref[:3]
            preds[zs[start // 128 + half], yv] = jax.nn.sigmoid(logit)

    for start in range(0, width, 256):
        cols = slice(start, start + 256)
        finish(0, start, matmul(w_ref[:, :576], g_ref[:576, cols]))
        cut = matmul(w_ref[:, :384], g_ref[192:576, cols])
        finish(2, start, cut)
        finish(1, start, cut + matmul(w_ref[:, 832:1024], g_ref[576:768, cols]))
        cut = matmul(w_ref[:, 640:1024], g_ref[576:960, cols])
        finish(3, start, cut)
        finish(4, start, cut + matmul(w_ref[:, :192], g_ref[384:576, cols]))
        finish(5, start, matmul(w_ref[:, :576], g_ref[576:1152, cols]))
    return preds


def weighted(preds, totals):
    zweights, yweights = variant_weights("gz")[0], variant_weights("xy")[0]
    for (zv, yv), pred in preds.items():
        at = VARIANTS[zv][0] * CORE + VARIANTS[yv][0]
        term = pred * (zweights[zv] * yweights[yv])
        totals[at] = term if at not in totals else totals[at] + term
    return totals


def inner_kernel(f_ref, ylo_ref, yhi_ref, w_ref, bias_ref, hw_ref, hb_ref, sums_ref, g_ref):
    def cell(y, z):
        return ylo_ref[0, z - 1] if y == 0 else (yhi_ref[0, z - 1] if y == 5 else f_ref[y - 1, z - 1])

    preds = predictions(INNER, cell, w_ref, bias_ref, hw_ref, hb_ref, g_ref)
    for at, total in weighted(preds, {}).items():
        sums_ref[at, :3] = total


def outer_kernel(
    f_ref, ylo_ref, yhi_ref, zlo_ref, zhi_ref, w_ref, bias_ref, hw_ref, hb_ref, sums_ref, a_ref, col_ref,
    out_ref, table_ref, g_ref, b_ref,
):
    def cell(y, z):
        if z == 0 or z == 5:
            return (zlo_ref if z == 0 else zhi_ref)[y, 0]
        return ylo_ref[0, z - 1] if y == 0 else (yhi_ref[0, z - 1] if y == 5 else f_ref[y - 1, z - 1])

    preds = predictions(OUTER, cell, w_ref, bias_ref, hw_ref, hb_ref, g_ref)
    totals = weighted(preds, {at: sums_ref[at, :3] for at in range(16) if at // CORE in (1, 2)})
    zcover, ycover = variant_weights("gz")[1], variant_weights("xy")[1]
    for at in range(16):
        blend = totals[at] / (zcover[at // CORE] * ycover[at % CORE])
        for a in range(3):
            out_ref[a * 16 + at : a * 16 + at + 1, :] = blend[a : a + 1]
    count = lax.broadcasted_iota(jnp.int32, (256, 128), 0).astype(jnp.float32).astype(jnp.bfloat16)
    none = jnp.zeros((), jnp.bfloat16)
    for r in range(48):
        value = out_ref[r : r + 1].astype(jnp.bfloat16)
        here = count == col_ref[r : r + 1].astype(jnp.bfloat16)
        b_ref[:, r * 128 : r * 128 + 128] = jnp.where(here, value, none)
    both = lax.dot_general(
        a_ref[...], b_ref[...], (((1,), (1,)), ((), ())), preferred_element_type=jnp.float32
    )
    table_ref[:256] = both[:, :128].astype(jnp.bfloat16)
    table_ref[256:] = both[:, 128:].astype(jnp.bfloat16)


def vmem(count):
    return [pl.BlockSpec(memory_space=pltpu.VMEM)] * count


def shape(dims, dtype):
    return jax.ShapeDtypeStruct(dims, dtype)


def in_hbm(array):
    return pltpu.with_memory_space_constraint(array, pltpu.HBM)


def arrange(features):
    yface, zface = shape((1, CORE, 64, 128), jnp.bfloat16), shape((CORE, 1, 64, 128), jnp.bfloat16)
    return pl.pallas_call(
        arrange_kernel,
        out_shape=(shape((CORE, CORE, 64, 128), jnp.bfloat16), yface, yface, zface, zface),
        in_specs=[pl.BlockSpec(memory_space=pltpu.HBM)],
        out_specs=tuple(vmem(5)),
        scratch_shapes=[
            pltpu.VMEM((1024, 128), jnp.float32), pltpu.VMEM((1024, 128), jnp.bfloat16), pltpu.SemaphoreType.DMA(()),
        ],
        compiler_params=pltpu.CompilerParams(vmem_limit_bytes=VMEM_LIMIT),
        name="arrange",
    )(in_hbm(features))


def prepare(*operands):
    return pl.pallas_call(
        prepare_kernel,
        out_shape=(
            shape((256, 6144), jnp.bfloat16), shape((48, 128), jnp.float32), shape((192, 1024), jnp.bfloat16),
            shape((64, 128), jnp.float32), shape((8, 128), jnp.float32), shape((3, 64), jnp.bfloat16),
        ),
        in_specs=[pl.BlockSpec(memory_space=pltpu.HBM)] * 7,
        out_specs=tuple(vmem(6)),
        scratch_shapes=[pltpu.VMEM(o.shape, o.dtype) for o in operands[:-1]]
        + [pltpu.VMEM((48, 128), jnp.float32), pltpu.SemaphoreType.DMA((7,))],
        compiler_params=pltpu.CompilerParams(vmem_limit_bytes=VMEM_LIMIT),
        cost_estimate=pl.CostEstimate(flops=10**9, bytes_accessed=10**7, transcendentals=0),
        name="prepare",
    )(*map(in_hbm, operands))


def inner(*operands):
    return pl.pallas_call(
        inner_kernel,
        out_shape=shape((16, 8, 128), jnp.float32),
        in_specs=vmem(7),
        out_specs=vmem(1)[0],
        scratch_shapes=[pltpu.VMEM((6 * 192, 512), jnp.bfloat16)],
        compiler_params=pltpu.CompilerParams(vmem_limit_bytes=VMEM_LIMIT),
        cost_estimate=pl.CostEstimate(flops=2 * 10**9, bytes_accessed=10**6, transcendentals=0),
        name="inner",
    )(*operands)


def outer(*operands):
    return pl.pallas_call(
        outer_kernel,
        out_shape=(shape((48, 128), jnp.float32), shape((512, 128), jnp.bfloat16)),
        in_specs=vmem(12),
        out_specs=tuple(vmem(2)),
        scratch_shapes=[pltpu.VMEM((6 * 192, 256), jnp.bfloat16), pltpu.VMEM((256, 6144), jnp.bfloat16)],
        compiler_params=pltpu.CompilerParams(vmem_limit_bytes=VMEM_LIMIT),
        name="outer",
    )(*operands)


def on_device(features, conv_w, conv_b, head_w, head_b, bins, edge_ids, owner_map):
    gz_peers, xy_peers = lax.axis_size("gz"), lax.axis_size("xy")
    cells, yfirst, ylast, zfirst, zlast = arrange(features.reshape(1024, 128))
    ylo, yhi = neighbours("xy", yfirst, ylast)
    owners, columns, weights, bias, offset, heads = prepare(
        edge_ids.reshape(48, 128), bins.reshape(16, 128), owner_map.reshape(32, 128),
        jnp.transpose(conv_w, (2, 3, 4, 0, 1)), conv_b.reshape(1, 64), head_b.reshape(1, 3), head_w,
    )
    first = jnp.concatenate([ylo[:, :1], zfirst, yhi[:, :1]], axis=0)
    last = jnp.concatenate([ylo[:, CORE - 1 :], zlast, yhi[:, CORE - 1 :]], axis=0)
    zlo, zhi = neighbours("gz", first, last)
    sums = inner(cells, ylo, yhi, weights, bias, heads, offset)
    blended, table = outer(cells, ylo, yhi, zlo, zhi, weights, bias, heads, offset, sums, owners, columns)
    parts = lax.all_to_all(table.reshape(gz_peers, xy_peers, 128), "gz", 0, 0, tiled=True)
    sums = jnp.sum(parts.astype(jnp.float32), axis=0)
    share = jnp.sum(lax.all_to_all(sums, "xy", 0, 0, tiled=True), axis=0, keepdims=True)
    return blended.reshape(3, CORE, CORE, 128), share


def solution(mesh):
    in_specs = (
        P(None, "gz", "xy", None),
        P(),
        P(),
        P(),
        P(),
        P("gz", "xy", None),
        P(None, "gz", "xy", None),
        P(),
    )
    out_specs = (P(None, "gz", "xy", None), P(("gz", "xy"), None))
    return jax.shard_map(
        on_device, mesh=mesh, in_specs=in_specs, out_specs=out_specs, check_vma=False
    )
```

```python
import jax
import jax.numpy as jnp
import numpy as np
from jax import lax
from jax.experimental import pallas as pl
from jax.experimental.pallas import tpu as pltpu
from jax.sharding import PartitionSpec as P

BINS = 16
CORE = 4
TAPS = 3
FULL = (0, 1, 2)
VMEM_LIMIT = 32 * 1024 * 1024

VARIANTS = ((0, FULL), (1, FULL), (1, (0, 1)), (2, (1, 2)), (2, FULL), (3, FULL))
INNER = (1, 2, 3, 4)
OUTER = (0, 5)
INNER_ROWS = [(axis, at) for axis in range(3) for at in range(4, 12)]
OUTER_ROWS = [(axis, at) for axis in range(3) for at in (0, 1, 2, 3, 12, 13, 14, 15)]


def swaps(axis, inside, outside):
    peers = lax.axis_size(axis)
    near = [(i, i ^ 1) for i in range(peers)]
    far = [(i, ((i + 1) ^ 1) - 1) for i in range(1, peers - 1)]
    return lax.ppermute(inside, axis, near), lax.ppermute(outside, axis, far)


def is_even(axis):
    return lax.axis_index(axis) % 2 == 0


def variant_weights(axis):
    index, total = lax.axis_index(axis), lax.axis_size(axis)
    lower = jnp.where(index > 0, 1.0, 0.0)
    upper = jnp.where(index < total - 1, 1.0, 0.0)
    weights = (3.0 + 2.0 * lower, 4.0, lower, upper, 4.0, 3.0 + 2.0 * upper)
    cover = (3.0 + 2.0 * lower, 4.0 + lower, 4.0 + upper, 3.0 + 2.0 * upper)
    return weights, cover


def column_of(row, size):
    length = row.shape[1]
    down = lax.broadcasted_iota(jnp.int32, (size, length), 0)
    along = lax.broadcasted_iota(jnp.int32, (size, length), 1)
    return jnp.broadcast_to(jnp.sum(jnp.where(down == along, row, 0.0), axis=1, keepdims=True), (size, 128))


def arrange_kernel(f_ref, cells_ref, ynear_ref, yfar_ref, znear_ref, zfar_ref, wide, f_v, sem):
    copy = pltpu.make_async_copy(f_ref, f_v, sem)
    copy.start()
    copy.wait()
    wide[...] = f_v[...].astype(jnp.float32)
    cells = {}
    for y in range(CORE):
        for z in range(CORE):
            cells[y, z] = wide[pl.ds(z * CORE + y, 64, stride=16), :].astype(jnp.bfloat16)
            cells_ref[y, z] = cells[y, z]
    last = CORE - 1
    even = is_even("xy")
    for z in range(CORE):
        ynear_ref[0, z] = jnp.where(even, cells[last, z], cells[0, z])
        yfar_ref[0, z] = jnp.where(even, cells[0, z], cells[last, z])
    even = is_even("gz")
    for y in range(CORE):
        znear_ref[y, 0] = jnp.where(even, cells[y, last], cells[y, 0])
        zfar_ref[y, 0] = jnp.where(even, cells[y, 0], cells[y, last])


def prepare_kernel(
    ids_hbm, bins_hbm, map_hbm, taps_hbm, cb_hbm, hb_hbm, hw_hbm,
    a_ref, col_ref, w_ref, bias_ref, off_ref, hw_ref,
    ids_ref, bins_ref, map_ref, taps_ref, cb_ref, hb_ref, row_ref, sems,
):
    pairs = (
        (ids_hbm, ids_ref), (map_hbm, map_ref), (bins_hbm, bins_ref), (taps_hbm, taps_ref), (cb_hbm, cb_ref),
        (hb_hbm, hb_ref), (hw_hbm, hw_ref),
    )
    copies = [pltpu.make_async_copy(src, dst, sems.at[i]) for i, (src, dst) in enumerate(pairs)]
    for copy in copies:
        copy.start()
    for copy in copies:
        copy.wait()
    one = jnp.ones((), jnp.bfloat16)
    none = jnp.zeros((), jnp.bfloat16)
    bins = bins_ref[...]
    for block in range(6):
        rows = slice(block * 8, block * 8 + 8)
        ids = ids_ref[rows]
        edge = jnp.maximum(ids, 0)
        low = edge & 127
        high = edge >> 7
        slot = jnp.zeros((8, 128), jnp.int32)
        for h in range(32):
            line = jnp.broadcast_to(map_ref[h : h + 1], (8, 128))
            slot = jnp.where(high == h, jnp.take_along_axis(line, low, axis=1, mode="promise_in_bounds"), slot)
        owner = slot >> 3
        place = (owner & 384) + ((owner & 1) << 6) + ((owner >> 1) & 63)
        first = block % 2 * 8
        column = (place >> 8) * 128 + (slot & 7) * BINS + bins[first : first + 8]
        col_ref[rows] = jnp.where(ids >= 0, column, -1).astype(jnp.float32)
        row_ref[rows] = (place & 255).astype(jnp.float32)
    count = lax.broadcasted_iota(jnp.int32, (256, 128), 0).astype(jnp.float32).astype(jnp.bfloat16)
    for i, (axis, at) in enumerate(INNER_ROWS + OUTER_ROWS):
        r = axis * 16 + at
        row = row_ref[r : r + 1].astype(jnp.bfloat16)
        a_ref[:, i * 128 : i * 128 + 128] = jnp.where(count == row, one, none)
    for dx in range(TAPS):
        rows = jnp.concatenate([taps_ref[t % 3, t // 3, dx] for t in range(9)], axis=1)
        w_ref[64 * dx : 64 * dx + 64, :576] = rows
        w_ref[64 * dx : 64 * dx + 64, 640:1024] = rows[:, 192:]
    bias_ref[...] = column_of(cb_ref[...], 64)
    off_ref[...] = column_of(hb_ref[...], 8)


def predictions(zs, cell, w_ref, bias_ref, hw_ref, hb_ref, g_ref):
    width = 128 * len(zs)
    zero = jnp.zeros((64, 128), jnp.bfloat16)
    for y in range(6):
        for dz in range(TAPS):
            for i, v in enumerate(zs):
                z, kept = VARIANTS[v]
                part = cell(y, z + dz) if dz in kept else zero
                g_ref[(y * 3 + dz) * 64 : (y * 3 + dz) * 64 + 64, i * 128 : i * 128 + 128] = part
    lane = lax.broadcasted_iota(jnp.int32, (64, 128), 1)
    bias = bias_ref[...]
    preds = {}

    def matmul(left, right):
        return lax.dot_general(left, right, (((1,), (0,)), ((), ())), preferred_element_type=jnp.float32)

    def finish(yv, start, p):
        hidden = []
        for half in range(2):
            q = p[:, half * 128 : half * 128 + 128]
            before = jnp.where(lane == 0, 0.0, pltpu.roll(q[:64], 1, 1))
            after = jnp.where(lane == 127, 0.0, pltpu.roll(q[128:], 127, 1))
            pre = before + q[64:128] + after
            hidden.append(jnp.maximum(pre + bias, 0.0).astype(jnp.bfloat16))
        logits = matmul(hw_ref[...], jnp.concatenate(hidden, axis=1))
        for half in range(2):
            logit = logits[:, half * 128 : half * 128 + 128] + hb_ref[:3]
            preds[zs[start // 128 + half], yv] = jax.nn.sigmoid(logit)

    for start in range(0, width, 256):
        cols = slice(start, start + 256)
        finish(0, start, matmul(w_ref[:, :576], g_ref[:576, cols]))
        cut = matmul(w_ref[:, :384], g_ref[192:576, cols])
        finish(2, start, cut)
        finish(1, start, cut + matmul(w_ref[:, 832:1024], g_ref[576:768, cols]))
        cut = matmul(w_ref[:, 640:1024], g_ref[576:960, cols])
        finish(3, start, cut)
        finish(4, start, cut + matmul(w_ref[:, :192], g_ref[384:576, cols]))
        finish(5, start, matmul(w_ref[:, :576], g_ref[576:1152, cols]))
    return preds


def blend(preds):
    zweights, zcover = variant_weights("gz")
    yweights, ycover = variant_weights("xy")
    totals = {}
    for (zv, yv), pred in preds.items():
        at = VARIANTS[zv][0] * CORE + VARIANTS[yv][0]
        term = pred * (zweights[zv] * yweights[yv])
        totals[at] = term if at not in totals else totals[at] + term
    return {at: total / (zcover[at // CORE] * ycover[at % CORE]) for at, total in totals.items()}


def histogram(rows, value_ref, col_ref, a_ref, b_ref):
    count = lax.broadcasted_iota(jnp.int32, (256, 128), 0).astype(jnp.float32).astype(jnp.bfloat16)
    none = jnp.zeros((), jnp.bfloat16)
    for i, (axis, at) in enumerate(rows):
        r = axis * 16 + at
        here = count == col_ref[r : r + 1].astype(jnp.bfloat16)
        b_ref[:, i * 128 : i * 128 + 128] = jnp.where(here, value_ref[i : i + 1].astype(jnp.bfloat16), none)
    return lax.dot_general(a_ref, b_ref[...], (((1,), (1,)), ((), ())), preferred_element_type=jnp.float32)


def edges(near_ref, far_ref, axis):
    even = is_even(axis)

    def low(*at):
        return jnp.where(even, far_ref[at], near_ref[at])

    def high(*at):
        return jnp.where(even, near_ref[at], far_ref[at])

    return low, high


def inner_kernel(
    f_ref, ynear_ref, yfar_ref, w_ref, bias_ref, hw_ref, hb_ref, a_ref, col_ref, part_ref, counts_ref, g_ref, b_ref
):
    ylow, yhigh = edges(ynear_ref, yfar_ref, "xy")

    def cell(y, z):
        return ylow(0, z - 1) if y == 0 else (yhigh(0, z - 1) if y == 5 else f_ref[y - 1, z - 1])

    blends = blend(predictions(INNER, cell, w_ref, bias_ref, hw_ref, hb_ref, g_ref))
    for i, (axis, at) in enumerate(INNER_ROWS):
        part_ref[i : i + 1] = blends[at][axis : axis + 1]
    counts_ref[...] = histogram(INNER_ROWS, part_ref, col_ref, a_ref[:, : 24 * 128], b_ref)


def outer_kernel(
    f_ref, ynear_ref, yfar_ref, znear_ref, zfar_ref, w_ref, bias_ref, hw_ref, hb_ref, a_ref, col_ref, part_ref, counts_ref,
    out_ref, table_ref, g_ref, b_ref, value_ref,
):
    ylow, yhigh = edges(ynear_ref, yfar_ref, "xy")
    zlow, zhigh = edges(znear_ref, zfar_ref, "gz")

    def cell(y, z):
        if z == 0 or z == 5:
            return (zlow if z == 0 else zhigh)(y, 0)
        return ylow(0, z - 1) if y == 0 else (yhigh(0, z - 1) if y == 5 else f_ref[y - 1, z - 1])

    blends = blend(predictions(OUTER, cell, w_ref, bias_ref, hw_ref, hb_ref, g_ref))
    for i, (axis, at) in enumerate(OUTER_ROWS):
        value_ref[i : i + 1] = blends[at][axis : axis + 1]
    for axis in range(3):
        out_ref[axis * 16 : axis * 16 + 4] = value_ref[axis * 8 : axis * 8 + 4]
        out_ref[axis * 16 + 4 : axis * 16 + 12] = part_ref[axis * 8 : axis * 8 + 8]
        out_ref[axis * 16 + 12 : axis * 16 + 16] = value_ref[axis * 8 + 4 : axis * 8 + 8]
    both = counts_ref[...] + histogram(OUTER_ROWS, value_ref, col_ref, a_ref[:, 24 * 128 :], b_ref)
    table_ref[:256] = both[:, :128].astype(jnp.bfloat16)
    table_ref[256:] = both[:, 128:].astype(jnp.bfloat16)


def vmem(count):
    return [pl.BlockSpec(memory_space=pltpu.VMEM)] * count


def shape(dims, dtype):
    return jax.ShapeDtypeStruct(dims, dtype)


def in_hbm(array):
    return pltpu.with_memory_space_constraint(array, pltpu.HBM)


def arrange(features):
    yface, zface = shape((1, CORE, 64, 128), jnp.bfloat16), shape((CORE, 1, 64, 128), jnp.bfloat16)
    return pl.pallas_call(
        arrange_kernel,
        out_shape=(shape((CORE, CORE, 64, 128), jnp.bfloat16), yface, yface, zface, zface),
        in_specs=[pl.BlockSpec(memory_space=pltpu.HBM)],
        out_specs=tuple(vmem(5)),
        scratch_shapes=[
            pltpu.VMEM((1024, 128), jnp.float32), pltpu.VMEM((1024, 128), jnp.bfloat16), pltpu.SemaphoreType.DMA(()),
        ],
        compiler_params=pltpu.CompilerParams(vmem_limit_bytes=VMEM_LIMIT),
        name="arrange",
    )(in_hbm(features))


def prepare(*operands):
    return pl.pallas_call(
        prepare_kernel,
        out_shape=(
            shape((256, 6144), jnp.bfloat16), shape((48, 128), jnp.float32), shape((192, 1024), jnp.bfloat16),
            shape((64, 128), jnp.float32), shape((8, 128), jnp.float32), shape((3, 64), jnp.bfloat16),
        ),
        in_specs=[pl.BlockSpec(memory_space=pltpu.HBM)] * 7,
        out_specs=tuple(vmem(6)),
        scratch_shapes=[pltpu.VMEM(o.shape, o.dtype) for o in operands[:-1]]
        + [pltpu.VMEM((48, 128), jnp.float32), pltpu.SemaphoreType.DMA((7,))],
        compiler_params=pltpu.CompilerParams(vmem_limit_bytes=VMEM_LIMIT),
        cost_estimate=pl.CostEstimate(flops=10**9, bytes_accessed=10**7, transcendentals=0),
        name="prepare",
    )(*map(in_hbm, operands))


def inner(*operands):
    return pl.pallas_call(
        inner_kernel,
        out_shape=(shape((24, 128), jnp.float32), shape((256, 256), jnp.float32)),
        in_specs=vmem(9),
        out_specs=tuple(vmem(2)),
        scratch_shapes=[pltpu.VMEM((6 * 192, 512), jnp.bfloat16), pltpu.VMEM((256, 3072), jnp.bfloat16)],
        compiler_params=pltpu.CompilerParams(vmem_limit_bytes=VMEM_LIMIT),
        cost_estimate=pl.CostEstimate(flops=2 * 10**9, bytes_accessed=10**6, transcendentals=0),
        name="inner",
    )(*operands)


def outer(*operands):
    return pl.pallas_call(
        outer_kernel,
        out_shape=(shape((48, 128), jnp.float32), shape((512, 128), jnp.bfloat16)),
        in_specs=vmem(13),
        out_specs=tuple(vmem(2)),
        scratch_shapes=[
            pltpu.VMEM((6 * 192, 256), jnp.bfloat16), pltpu.VMEM((256, 3072), jnp.bfloat16),
            pltpu.VMEM((24, 128), jnp.float32),
        ],
        compiler_params=pltpu.CompilerParams(vmem_limit_bytes=VMEM_LIMIT),
        name="outer",
    )(*operands)


def groups(kept):
    ids = np.arange(512).reshape(4, 8, 8, 2)
    return ids.transpose(1, 2, 0, 3).reshape(64, 8).tolist() if kept == "xc" else ids.transpose(0, 3, 1, 2).reshape(8, 64).tolist()


def on_device(features, conv_w, conv_b, head_w, head_b, bins, edge_ids, owner_map):
    last = CORE - 1
    cells, ynear, yfar, znear, zfar = arrange(features.reshape(1024, 128))
    ynear, yfar = swaps("xy", ynear, yfar)
    owners, columns, weights, bias, offset, heads = prepare(
        edge_ids.reshape(48, 128), bins.reshape(16, 128), owner_map.reshape(32, 128),
        jnp.transpose(conv_w, (2, 3, 4, 0, 1)), conv_b.reshape(1, 64), head_b.reshape(1, 3), head_w,
    )
    yeven, zeven = is_even("xy"), is_even("gz")
    ylow, yhigh = jnp.where(yeven, yfar, ynear), jnp.where(yeven, ynear, yfar)

    def with_corners(face, even):
        low = jnp.where(even, ylow[:, last:], ylow[:, :1])
        high = jnp.where(even, yhigh[:, last:], yhigh[:, :1])
        return jnp.concatenate([low, face, high], axis=0)

    znear, zfar = swaps("gz", with_corners(znear, zeven), with_corners(zfar, jnp.logical_not(zeven)))
    part, counts = inner(cells, ynear, yfar, weights, bias, heads, offset, owners, columns)
    blended, table = outer(
        cells, ynear, yfar, znear, zfar, weights, bias, heads, offset, owners, columns, part, counts
    )
    every = ("gz", "xy")
    parts = lax.all_to_all(table.reshape(8, 64, 128), every, 0, 0, tiled=True, axis_index_groups=groups("xc"))
    sums = jnp.sum(parts.astype(jnp.float32), axis=0)
    sums = lax.all_to_all(sums, every, 0, 0, tiled=True, axis_index_groups=groups("yz"))
    share = jnp.sum(sums, axis=0, keepdims=True)
    return blended.reshape(3, CORE, CORE, 128), share


def solution(mesh):
    in_specs = (
        P(None, "gz", "xy", None),
        P(),
        P(),
        P(),
        P(),
        P("gz", "xy", None),
        P(None, "gz", "xy", None),
        P(),
    )
    out_specs = (P(None, "gz", "xy", None), P(("gz", "xy"), None))
    return jax.shard_map(
        on_device, mesh=mesh, in_specs=in_specs, out_specs=out_specs, check_vma=False
    )
```

```python
import jax
import jax.numpy as jnp
import numpy as np
from jax import lax
from jax.experimental import pallas as pl
from jax.experimental.pallas import tpu as pltpu
from jax.sharding import PartitionSpec as P

BINS = 16
CORE = 4
TAPS = 3
FULL = (0, 1, 2)
VMEM_LIMIT = 32 * 1024 * 1024

VARIANTS = ((0, FULL), (1, FULL), (1, (0, 1)), (2, (1, 2)), (2, FULL), (3, FULL))
INNER = (1, 2, 3, 4)
OUTER = (0, 5)
INNER_ROWS = [(axis, at) for axis in range(3) for at in range(4, 12)]
OUTER_ROWS = [(axis, at) for axis in range(3) for at in (0, 1, 2, 3, 12, 13, 14, 15)]


def swaps(axis, inside, outside):
    peers = lax.axis_size(axis)
    near = [(i, i ^ 1) for i in range(peers)]
    far = [(i, ((i + 1) ^ 1) - 1) for i in range(1, peers - 1)]
    return lax.ppermute(inside, axis, near), lax.ppermute(outside, axis, far)


def is_even(axis):
    return lax.axis_index(axis) % 2 == 0


def variant_weights(axis):
    index, total = lax.axis_index(axis), lax.axis_size(axis)
    lower = jnp.where(index > 0, 1.0, 0.0)
    upper = jnp.where(index < total - 1, 1.0, 0.0)
    weights = (3.0 + 2.0 * lower, 4.0, lower, upper, 4.0, 3.0 + 2.0 * upper)
    cover = (3.0 + 2.0 * lower, 4.0 + lower, 4.0 + upper, 3.0 + 2.0 * upper)
    return weights, cover


def column_of(row, size):
    length = row.shape[1]
    down = lax.broadcasted_iota(jnp.int32, (size, length), 0)
    along = lax.broadcasted_iota(jnp.int32, (size, length), 1)
    return jnp.broadcast_to(jnp.sum(jnp.where(down == along, row, 0.0), axis=1, keepdims=True), (size, 128))


def arrange_kernel(f_ref, cells_ref, ynear_ref, yfar_ref, znear_ref, zfar_ref, wide, f_v, sems):
    parts = [slice(i * 256, i * 256 + 256) for i in range(4)]
    copies = [pltpu.make_async_copy(f_ref.at[part], f_v.at[part], sems.at[i]) for i, part in enumerate(parts)]
    for copy in copies:
        copy.start()
    for i, part in enumerate(parts):
        copies[i].wait()
        wide[part] = f_v[part].astype(jnp.float32)
        for y in range(CORE):
            for z in range(CORE):
                piece = wide[pl.ds(i * 256 + z * CORE + y, 16, stride=16), :].astype(jnp.bfloat16)
                cells_ref[y, z, i * 16 : i * 16 + 16] = piece
    cells = cells_ref
    last = CORE - 1
    even = is_even("xy")
    for z in range(CORE):
        ynear_ref[0, z] = jnp.where(even, cells[last, z], cells[0, z])
        yfar_ref[0, z] = jnp.where(even, cells[0, z], cells[last, z])
    even = is_even("gz")
    for y in range(CORE):
        znear_ref[y, 0] = jnp.where(even, cells[y, last], cells[y, 0])
        zfar_ref[y, 0] = jnp.where(even, cells[y, 0], cells[y, last])


def prepare_kernel(
    ids_hbm, bins_hbm, map_hbm, taps_hbm, cb_hbm, hb_hbm, hw_hbm,
    a_ref, col_ref, w_ref, bias_ref, off_ref, heads_ref,
    ids_ref, bins_ref, map_ref, taps_ref, cb_ref, hb_ref, hw_ref, row_ref, sems,
):
    pairs = (
        (ids_hbm, ids_ref), (map_hbm, map_ref), (bins_hbm, bins_ref), (taps_hbm, taps_ref), (cb_hbm, cb_ref),
        (hb_hbm, hb_ref), (hw_hbm, hw_ref),
    )
    copies = [pltpu.make_async_copy(src, dst, sems.at[i]) for i, (src, dst) in enumerate(pairs)]
    for copy in copies:
        copy.start()
    for copy in copies:
        copy.wait()
    one = jnp.ones((), jnp.bfloat16)
    none = jnp.zeros((), jnp.bfloat16)
    bins = bins_ref[...]
    for block in range(6):
        rows = slice(block * 8, block * 8 + 8)
        ids = ids_ref[rows]
        edge = jnp.maximum(ids, 0)
        low = edge & 127
        high = edge >> 7
        slot = jnp.zeros((8, 128), jnp.int32)
        for h in range(32):
            line = jnp.broadcast_to(map_ref[h : h + 1], (8, 128))
            slot = jnp.where(high == h, jnp.take_along_axis(line, low, axis=1, mode="promise_in_bounds"), slot)
        owner = slot >> 3
        place = (owner & 384) + ((owner & 1) << 6) + ((owner >> 1) & 63)
        first = block % 2 * 8
        column = (place >> 8) * 128 + (slot & 7) * BINS + bins[first : first + 8]
        col_ref[rows] = jnp.where(ids >= 0, column, -1).astype(jnp.float32)
        row_ref[rows] = (place & 255).astype(jnp.float32)
    count = lax.broadcasted_iota(jnp.int32, (256, 128), 0).astype(jnp.float32).astype(jnp.bfloat16)
    for i, (axis, at) in enumerate(INNER_ROWS + OUTER_ROWS):
        r = axis * 16 + at
        row = row_ref[r : r + 1].astype(jnp.bfloat16)
        a_ref[:, i * 128 : i * 128 + 128] = jnp.where(count == row, one, none)
    for dx in range(TAPS):
        rows = jnp.concatenate([taps_ref[t % 3, t // 3, dx] for t in range(9)], axis=1)
        w_ref[64 * dx : 64 * dx + 64, :576] = rows
        w_ref[64 * dx : 64 * dx + 64, 640:1024] = rows[:, 192:]
    bias_ref[...] = column_of(cb_ref[...], 64)
    off_ref[...] = column_of(hb_ref[...], 8)
    head = jnp.concatenate([hw_ref[...].astype(jnp.float32), jnp.zeros((5, 64), jnp.float32)], axis=0)
    blank = jnp.zeros((8, 64), jnp.float32)
    lines = [jnp.concatenate([head if u == v else blank for u in range(4)], axis=1) for v in range(4)]
    heads_ref[...] = jnp.concatenate(lines, axis=0).astype(jnp.bfloat16)


def predictions(zs, cell, w_ref, bias_ref, heads_ref, hb_ref, g_ref):
    width = 128 * len(zs)
    zero = jnp.zeros((64, 128), jnp.bfloat16)
    for y in range(6):
        for dz in range(TAPS):
            for i, v in enumerate(zs):
                z, kept = VARIANTS[v]
                part = cell(y, z + dz) if dz in kept else zero
                g_ref[(y * 3 + dz) * 64 : (y * 3 + dz) * 64 + 64, i * 128 : i * 128 + 128] = part
    lane = lax.broadcasted_iota(jnp.int32, (64, 128), 1)
    bias = bias_ref[...]
    preds = {}

    def matmul(left, right):
        return lax.dot_general(left, right, (((1,), (0,)), ((), ())), preferred_element_type=jnp.float32)

    def activate(p):
        hidden = []
        for half in range(2):
            q = p[:, half * 128 : half * 128 + 128]
            before = jnp.where(lane == 0, 0.0, pltpu.roll(q[:64], 1, 1))
            after = jnp.where(lane == 127, 0.0, pltpu.roll(q[128:], 127, 1))
            pre = before + q[64:128] + after
            hidden.append(jnp.maximum(pre + bias, 0.0).astype(jnp.bfloat16))
        return jnp.concatenate(hidden, axis=1)

    def head(batch):
        hidden = jnp.concatenate([h for _, _, h in batch], axis=0)
        rows = len(batch)
        logits = matmul(heads_ref[: 8 * rows, : 64 * rows], hidden)
        for i, (yv, start, _) in enumerate(batch):
            for half in range(2):
                logit = logits[i * 8 : i * 8 + 3, half * 128 : half * 128 + 128] + hb_ref[:3]
                preds[zs[start // 128 + half], yv] = jax.nn.sigmoid(logit)

    batch = []
    for start in range(0, width, 256):
        cols = slice(start, start + 256)

        def finish(yv, p):
            batch.append((yv, start, activate(p)))
            if len(batch) == 4:
                head(batch)
                batch.clear()

        finish(0, matmul(w_ref[:, :576], g_ref[:576, cols]))
        cut = matmul(w_ref[:, :384], g_ref[192:576, cols])
        finish(2, cut)
        finish(1, cut + matmul(w_ref[:, 832:1024], g_ref[576:768, cols]))
        cut = matmul(w_ref[:, 640:1024], g_ref[576:960, cols])
        finish(3, cut)
        finish(4, cut + matmul(w_ref[:, :192], g_ref[384:576, cols]))
        finish(5, matmul(w_ref[:, :576], g_ref[576:1152, cols]))
    if batch:
        head(batch)
    return preds


def blend(preds):
    zweights, zcover = variant_weights("gz")
    yweights, ycover = variant_weights("xy")
    totals = {}
    for (zv, yv), pred in preds.items():
        at = VARIANTS[zv][0] * CORE + VARIANTS[yv][0]
        term = pred * (zweights[zv] * yweights[yv])
        totals[at] = term if at not in totals else totals[at] + term
    return {at: total / (zcover[at // CORE] * ycover[at % CORE]) for at, total in totals.items()}


def histogram(rows, value_ref, col_ref, a_ref, b_ref):
    count = lax.broadcasted_iota(jnp.int32, (256, 128), 0).astype(jnp.float32).astype(jnp.bfloat16)
    none = jnp.zeros((), jnp.bfloat16)
    for i, (axis, at) in enumerate(rows):
        r = axis * 16 + at
        here = count == col_ref[r : r + 1].astype(jnp.bfloat16)
        b_ref[:, i * 128 : i * 128 + 128] = jnp.where(here, value_ref[i : i + 1].astype(jnp.bfloat16), none)
    return lax.dot_general(a_ref, b_ref[...], (((1,), (1,)), ((), ())), preferred_element_type=jnp.float32)


def edges(near_ref, far_ref, axis):
    even = is_even(axis)

    def low(*at):
        return jnp.where(even, far_ref[at], near_ref[at])

    def high(*at):
        return jnp.where(even, near_ref[at], far_ref[at])

    return low, high


def inner_kernel(
    f_ref, yfar_ref, ynear_ref, w_ref, bias_ref, heads_ref, hb_ref, a_ref, col_ref, part_ref, counts_ref, g_ref, b_ref
):
    ylow, yhigh = edges(ynear_ref, yfar_ref, "xy")

    def cell(y, z):
        return ylow(0, z - 1) if y == 0 else (yhigh(0, z - 1) if y == 5 else f_ref[y - 1, z - 1])

    blends = blend(predictions(INNER, cell, w_ref, bias_ref, heads_ref, hb_ref, g_ref))
    for i, (axis, at) in enumerate(INNER_ROWS):
        part_ref[i : i + 1] = blends[at][axis : axis + 1]
    counts_ref[...] = histogram(INNER_ROWS, part_ref, col_ref, a_ref[:, : 24 * 128], b_ref)


def outer_kernel(
    f_ref, yfar_ref, ynear_ref, zfar_ref, znear_ref, w_ref, bias_ref, heads_ref, hb_ref, a_ref, col_ref, part_ref, counts_ref,
    out_ref, table_ref, g_ref, b_ref, value_ref,
):
    ylow, yhigh = edges(ynear_ref, yfar_ref, "xy")
    zlow, zhigh = edges(znear_ref, zfar_ref, "gz")

    def cell(y, z):
        if z == 0 or z == 5:
            return (zlow if z == 0 else zhigh)(y, 0)
        return ylow(0, z - 1) if y == 0 else (yhigh(0, z - 1) if y == 5 else f_ref[y - 1, z - 1])

    blends = blend(predictions(OUTER, cell, w_ref, bias_ref, heads_ref, hb_ref, g_ref))
    for i, (axis, at) in enumerate(OUTER_ROWS):
        value_ref[i : i + 1] = blends[at][axis : axis + 1]
    for axis in range(3):
        out_ref[axis * 16 : axis * 16 + 4] = value_ref[axis * 8 : axis * 8 + 4]
        out_ref[axis * 16 + 4 : axis * 16 + 12] = part_ref[axis * 8 : axis * 8 + 8]
        out_ref[axis * 16 + 12 : axis * 16 + 16] = value_ref[axis * 8 + 4 : axis * 8 + 8]
    both = counts_ref[...] + histogram(OUTER_ROWS, value_ref, col_ref, a_ref[:, 24 * 128 :], b_ref)
    table_ref[:256] = both[:, :128].astype(jnp.bfloat16)
    table_ref[256:] = both[:, 128:].astype(jnp.bfloat16)


def vmem(count):
    return [pl.BlockSpec(memory_space=pltpu.VMEM)] * count


def shape(dims, dtype):
    return jax.ShapeDtypeStruct(dims, dtype)


def in_hbm(array):
    return pltpu.with_memory_space_constraint(array, pltpu.HBM)


def arrange(features):
    yface, zface = shape((1, CORE, 64, 128), jnp.bfloat16), shape((CORE, 1, 64, 128), jnp.bfloat16)
    return pl.pallas_call(
        arrange_kernel,
        out_shape=(shape((CORE, CORE, 64, 128), jnp.bfloat16), yface, yface, zface, zface),
        in_specs=[pl.BlockSpec(memory_space=pltpu.HBM)],
        out_specs=tuple(vmem(5)),
        scratch_shapes=[
            pltpu.VMEM((1024, 128), jnp.float32), pltpu.VMEM((1024, 128), jnp.bfloat16), pltpu.SemaphoreType.DMA((4,)),
        ],
        compiler_params=pltpu.CompilerParams(vmem_limit_bytes=VMEM_LIMIT),
        name="arrange",
    )(in_hbm(features))


def prepare(*operands):
    return pl.pallas_call(
        prepare_kernel,
        out_shape=(
            shape((256, 6144), jnp.bfloat16), shape((48, 128), jnp.float32), shape((192, 1024), jnp.bfloat16),
            shape((64, 128), jnp.float32), shape((8, 128), jnp.float32), shape((32, 256), jnp.bfloat16),
        ),
        in_specs=[pl.BlockSpec(memory_space=pltpu.HBM)] * 7,
        out_specs=tuple(vmem(6)),
        scratch_shapes=[pltpu.VMEM(o.shape, o.dtype) for o in operands]
        + [pltpu.VMEM((48, 128), jnp.float32), pltpu.SemaphoreType.DMA((7,))],
        compiler_params=pltpu.CompilerParams(vmem_limit_bytes=VMEM_LIMIT),
        cost_estimate=pl.CostEstimate(flops=10**9, bytes_accessed=10**7, transcendentals=0),
        name="prepare",
    )(*map(in_hbm, operands))


def inner(*operands):
    return pl.pallas_call(
        inner_kernel,
        out_shape=(shape((24, 128), jnp.float32), shape((256, 256), jnp.float32)),
        in_specs=vmem(9),
        out_specs=tuple(vmem(2)),
        scratch_shapes=[pltpu.VMEM((6 * 192, 512), jnp.bfloat16), pltpu.VMEM((256, 3072), jnp.bfloat16)],
        compiler_params=pltpu.CompilerParams(vmem_limit_bytes=VMEM_LIMIT),
        cost_estimate=pl.CostEstimate(flops=2 * 10**9, bytes_accessed=10**6, transcendentals=0),
        name="inner",
    )(*operands)


def outer(*operands):
    return pl.pallas_call(
        outer_kernel,
        out_shape=(shape((48, 128), jnp.float32), shape((512, 128), jnp.bfloat16)),
        in_specs=vmem(13),
        out_specs=tuple(vmem(2)),
        scratch_shapes=[
            pltpu.VMEM((6 * 192, 256), jnp.bfloat16), pltpu.VMEM((256, 3072), jnp.bfloat16),
            pltpu.VMEM((24, 128), jnp.float32),
        ],
        compiler_params=pltpu.CompilerParams(vmem_limit_bytes=VMEM_LIMIT),
        name="outer",
    )(*operands)


def finish_kernel(values_ref, sums_ref, out_ref, share_ref):
    out_ref[...] = values_ref[...]
    share_ref[...] = jnp.sum(sums_ref[...], axis=0, keepdims=True)


def finish(*operands):
    return pl.pallas_call(
        finish_kernel,
        out_shape=(shape((48, 128), jnp.float32), shape((1, 128), jnp.float32)),
        in_specs=vmem(2),
        out_specs=tuple(vmem(2)),
        compiler_params=pltpu.CompilerParams(vmem_limit_bytes=2 * 1024 * 1024),
        name="finish",
    )(*operands)


def groups(kept):
    ids = np.arange(512).reshape(4, 8, 8, 2)
    return ids.transpose(1, 2, 0, 3).reshape(64, 8).tolist() if kept == "xc" else ids.transpose(0, 3, 1, 2).reshape(8, 64).tolist()


def on_device(features, conv_w, conv_b, head_w, head_b, bins, edge_ids, owner_map):
    last = CORE - 1
    cells, ynear, yfar, znear, zfar = arrange(features.reshape(1024, 128))
    ynear, yfar = swaps("xy", ynear, yfar)
    owners, columns, weights, bias, offset, heads = prepare(
        edge_ids.reshape(48, 128), bins.reshape(16, 128), owner_map.reshape(32, 128),
        jnp.transpose(conv_w, (2, 3, 4, 0, 1)), conv_b.reshape(1, 64), head_b.reshape(1, 3), head_w,
    )
    yeven, zeven = is_even("xy"), is_even("gz")
    ylow, yhigh = jnp.where(yeven, yfar, ynear), jnp.where(yeven, ynear, yfar)

    def with_corners(face, even):
        low = jnp.where(even, ylow[:, last:], ylow[:, :1])
        high = jnp.where(even, yhigh[:, last:], yhigh[:, :1])
        return jnp.concatenate([low, face, high], axis=0)

    znear, zfar = swaps("gz", with_corners(znear, zeven), with_corners(zfar, jnp.logical_not(zeven)))
    part, counts = inner(cells, yfar, ynear, weights, bias, heads, offset, owners, columns)
    blended, table = outer(
        cells, yfar, ynear, zfar, znear, weights, bias, heads, offset, owners, columns, part, counts
    )
    every = ("gz", "xy")
    parts = lax.all_to_all(table.reshape(8, 64, 128), every, 0, 0, tiled=True, axis_index_groups=groups("xc"))
    sums = jnp.sum(parts.astype(jnp.float32), axis=0)
    sums = lax.all_to_all(sums, every, 0, 0, tiled=True, axis_index_groups=groups("yz"))
    blended, share = finish(blended, sums)
    return blended.reshape(3, CORE, CORE, 128), share


def solution(mesh):
    in_specs = (
        P(None, "gz", "xy", None),
        P(),
        P(),
        P(),
        P(),
        P("gz", "xy", None),
        P(None, "gz", "xy", None),
        P(),
    )
    out_specs = (P(None, "gz", "xy", None), P(("gz", "xy"), None))
    return jax.shard_map(
        on_device, mesh=mesh, in_specs=in_specs, out_specs=out_specs, check_vma=False
    )
```

```python
import jax
import jax.numpy as jnp
import numpy as np
from jax import lax
from jax.experimental import pallas as pl
from jax.experimental.pallas import tpu as pltpu
from jax.sharding import PartitionSpec as P

BINS = 16
CORE = 4
TAPS = 3
SMALL = 6
FULL = (0, 1, 2)
VMEM_LIMIT = 32 * 1024 * 1024

VARIANTS = ((0, FULL), (1, FULL), (1, (0, 1)), (2, (1, 2)), (2, FULL), (3, FULL))
FIELDS = {"x": (7, 2), "y": (4, 3), "z": (1, 3), "c": (0, 1)}
EXCHANGES = ("xc", "yz")
INNER = (1, 2, 3, 4)
OUTER = (0, 5)
INNER_ROWS = [(axis, at) for axis in range(3) for at in range(4, 12)]
OUTER_ROWS = [(axis, at) for axis in range(3) for at in (0, 1, 2, 3, 12, 13, 14, 15)]


def swaps(axis, inside, outside):
    peers = lax.axis_size(axis)
    near = [(i, i ^ 1) for i in range(peers)]
    far = [(i, ((i + 1) ^ 1) - 1) for i in range(1, peers - 1)]
    return lax.ppermute(inside, axis, near), lax.ppermute(outside, axis, far)


def is_even(axis):
    return lax.axis_index(axis) % 2 == 0


def variant_weights(axis):
    index, total = lax.axis_index(axis), lax.axis_size(axis)
    lower = jnp.where(index > 0, 1.0, 0.0)
    upper = jnp.where(index < total - 1, 1.0, 0.0)
    weights = (3.0 + 2.0 * lower, 4.0, lower, upper, 4.0, 3.0 + 2.0 * upper)
    cover = (3.0 + 2.0 * lower, 4.0 + lower, 4.0 + upper, 3.0 + 2.0 * upper)
    return weights, cover


def column_of(row, size):
    length = row.shape[1]
    down = lax.broadcasted_iota(jnp.int32, (size, length), 0)
    along = lax.broadcasted_iota(jnp.int32, (size, length), 1)
    return jnp.broadcast_to(jnp.sum(jnp.where(down == along, row, 0.0), axis=1, keepdims=True), (size, 128))


def arrange_kernel(f_ref, *refs):
    sources, refs = refs[:SMALL], refs[SMALL:]
    (cells_ref, ynear_ref, yfar_ref, znear_ref, zfar_ref), refs = refs[:5], refs[5:]
    targets, (wide, f_v, sems) = refs[:SMALL], refs[SMALL:]
    parts = [slice(i * 256, i * 256 + 256) for i in range(4)]
    copies = [pltpu.make_async_copy(f_ref.at[part], f_v.at[part], sems.at[i]) for i, part in enumerate(parts)]
    copies += [pltpu.make_async_copy(src, dst, sems.at[4 + i]) for i, (src, dst) in enumerate(zip(sources, targets))]
    for copy in copies:
        copy.start()
    for i, part in enumerate(parts):
        copies[i].wait()
        wide[part] = f_v[part].astype(jnp.float32)
        for y in range(CORE):
            for z in range(CORE):
                piece = wide[pl.ds(i * 256 + z * CORE + y, 16, stride=16), :].astype(jnp.bfloat16)
                cells_ref[y, z, i * 16 : i * 16 + 16] = piece
    cells = cells_ref
    last = CORE - 1
    even = is_even("xy")
    for z in range(CORE):
        ynear_ref[0, z] = jnp.where(even, cells[last, z], cells[0, z])
        yfar_ref[0, z] = jnp.where(even, cells[0, z], cells[last, z])
    even = is_even("gz")
    for y in range(CORE):
        znear_ref[y, 0] = jnp.where(even, cells[y, last], cells[y, 0])
        zfar_ref[y, 0] = jnp.where(even, cells[y, 0], cells[y, last])
    for copy in copies[4:]:
        copy.wait()


def prepare_kernel(
    taps_hbm, cb_ref, hb_ref, hw_ref, ids_ref, bins_ref, map_ref, w_ref, bias_ref, off_ref, heads_ref, a_ref, col_ref,
    row_ref, taps_ref, sem,
):
    fetch = pltpu.make_async_copy(taps_hbm, taps_ref, sem)
    fetch.start()
    lookup(ids_ref, bins_ref, map_ref, a_ref, col_ref, row_ref)
    fetch.wait()
    for dx in range(TAPS):
        rows = jnp.concatenate([taps_ref[t % 3, t // 3, dx] for t in range(9)], axis=1)
        w_ref[64 * dx : 64 * dx + 64, :576] = rows
        w_ref[64 * dx : 64 * dx + 64, 640:1024] = rows[:, 192:]
    bias_ref[...] = column_of(cb_ref[...], 64)
    off_ref[...] = column_of(hb_ref[...], 8)
    head = jnp.concatenate([hw_ref[...].astype(jnp.float32), jnp.zeros((5, 64), jnp.float32)], axis=0)
    blank = jnp.zeros((8, 64), jnp.float32)
    lines = [jnp.concatenate([head if u == v else blank for u in range(4)], axis=1) for v in range(4)]
    heads_ref[...] = jnp.concatenate(lines, axis=0).astype(jnp.bfloat16)


def lookup(ids_ref, bins_ref, map_ref, a_ref, col_ref, row_ref):
    one = jnp.ones((), jnp.bfloat16)
    none = jnp.zeros((), jnp.bfloat16)
    bins = bins_ref[...]
    for block in range(6):
        rows = slice(block * 8, block * 8 + 8)
        ids = ids_ref[rows]
        edge = jnp.maximum(ids, 0)
        low = edge & 127
        high = edge >> 7
        slot = jnp.zeros((8, 128), jnp.int32)
        for h in range(32):
            line = jnp.broadcast_to(map_ref[h : h + 1], (8, 128))
            slot = jnp.where(high == h, jnp.take_along_axis(line, low, axis=1, mode="promise_in_bounds"), slot)
        owner = slot >> 3
        place, shift = 0, 9
        for axis in "".join(EXCHANGES):
            low, width = FIELDS[axis]
            shift -= width
            place += ((owner >> low) & (2**width - 1)) << shift
        first = block % 2 * 8
        column = (place >> 8) * 128 + (slot & 7) * BINS + bins[first : first + 8]
        col_ref[rows] = jnp.where(ids >= 0, column, -1).astype(jnp.float32)
        row_ref[rows] = (place & 255).astype(jnp.float32)
    count = lax.broadcasted_iota(jnp.int32, (256, 128), 0).astype(jnp.float32).astype(jnp.bfloat16)
    for i, (axis, at) in enumerate(INNER_ROWS + OUTER_ROWS):
        r = axis * 16 + at
        row = row_ref[r : r + 1].astype(jnp.bfloat16)
        a_ref[:, i * 128 : i * 128 + 128] = jnp.where(count == row, one, none)


def predictions(zs, cell, w_ref, bias_ref, heads_ref, hb_ref, g_ref):
    width = 128 * len(zs)
    zero = jnp.zeros((64, 128), jnp.bfloat16)
    for y in range(6):
        for dz in range(TAPS):
            for i, v in enumerate(zs):
                z, kept = VARIANTS[v]
                part = cell(y, z + dz) if dz in kept else zero
                g_ref[(y * 3 + dz) * 64 : (y * 3 + dz) * 64 + 64, i * 128 : i * 128 + 128] = part
    lane = lax.broadcasted_iota(jnp.int32, (64, 128), 1)
    bias = bias_ref[...]
    preds = {}

    def matmul(left, right):
        return lax.dot_general(left, right, (((1,), (0,)), ((), ())), preferred_element_type=jnp.float32)

    def activate(p):
        hidden = []
        for half in range(2):
            q = p[:, half * 128 : half * 128 + 128]
            before = jnp.where(lane == 0, 0.0, pltpu.roll(q[:64], 1, 1))
            after = jnp.where(lane == 127, 0.0, pltpu.roll(q[128:], 127, 1))
            pre = before + q[64:128] + after
            hidden.append(jnp.maximum(pre + bias, 0.0).astype(jnp.bfloat16))
        return jnp.concatenate(hidden, axis=1)

    def head(batch):
        hidden = jnp.concatenate([h for _, _, h in batch], axis=0)
        rows = len(batch)
        logits = matmul(heads_ref[: 8 * rows, : 64 * rows], hidden)
        for i, (yv, start, _) in enumerate(batch):
            for half in range(2):
                logit = logits[i * 8 : i * 8 + 3, half * 128 : half * 128 + 128] + hb_ref[:3]
                preds[zs[start // 128 + half], yv] = jax.nn.sigmoid(logit)

    batch = []
    for start in range(0, width, 256):
        cols = slice(start, start + 256)

        def finish(yv, p):
            batch.append((yv, start, activate(p)))
            if len(batch) == 4:
                head(batch)
                batch.clear()

        finish(0, matmul(w_ref[:, :576], g_ref[:576, cols]))
        cut = matmul(w_ref[:, :384], g_ref[192:576, cols])
        finish(2, cut)
        finish(1, cut + matmul(w_ref[:, 832:1024], g_ref[576:768, cols]))
        cut = matmul(w_ref[:, 640:1024], g_ref[576:960, cols])
        finish(3, cut)
        finish(4, cut + matmul(w_ref[:, :192], g_ref[384:576, cols]))
        finish(5, matmul(w_ref[:, :576], g_ref[576:1152, cols]))
    if batch:
        head(batch)
    return preds


def blend(preds):
    zweights, zcover = variant_weights("gz")
    yweights, ycover = variant_weights("xy")
    totals = {}
    for (zv, yv), pred in preds.items():
        at = VARIANTS[zv][0] * CORE + VARIANTS[yv][0]
        term = pred * (zweights[zv] * yweights[yv])
        totals[at] = term if at not in totals else totals[at] + term
    return {at: total / (zcover[at // CORE] * ycover[at % CORE]) for at, total in totals.items()}


def histogram(rows, value_ref, col_ref, a_ref, b_ref):
    count = lax.broadcasted_iota(jnp.int32, (256, 128), 0).astype(jnp.float32).astype(jnp.bfloat16)
    none = jnp.zeros((), jnp.bfloat16)
    for i, (axis, at) in enumerate(rows):
        r = axis * 16 + at
        here = count == col_ref[r : r + 1].astype(jnp.bfloat16)
        b_ref[:, i * 128 : i * 128 + 128] = jnp.where(here, value_ref[i : i + 1].astype(jnp.bfloat16), none)
    return lax.dot_general(a_ref, b_ref[...], (((1,), (1,)), ((), ())), preferred_element_type=jnp.float32)


def edges(near_ref, far_ref, axis):
    even = is_even(axis)

    def low(*at):
        return jnp.where(even, far_ref[at], near_ref[at])

    def high(*at):
        return jnp.where(even, near_ref[at], far_ref[at])

    return low, high


def inner_kernel(
    f_ref, yfar_ref, ynear_ref, w_ref, bias_ref, heads_ref, hb_ref, a_ref, col_ref, part_ref, counts_ref, g_ref, b_ref
):
    ylow, yhigh = edges(ynear_ref, yfar_ref, "xy")

    def cell(y, z):
        return ylow(0, z - 1) if y == 0 else (yhigh(0, z - 1) if y == 5 else f_ref[y - 1, z - 1])

    blends = blend(predictions(INNER, cell, w_ref, bias_ref, heads_ref, hb_ref, g_ref))
    for i, (axis, at) in enumerate(INNER_ROWS):
        part_ref[i : i + 1] = blends[at][axis : axis + 1]
    counts_ref[...] = histogram(INNER_ROWS, part_ref, col_ref, a_ref[:, : 24 * 128], b_ref)


def outer_kernel(
    f_ref, yfar_ref, ynear_ref, zfar_ref, znear_ref, w_ref, bias_ref, heads_ref, hb_ref, a_ref, col_ref, part_ref, counts_ref,
    out_ref, table_ref, g_ref, b_ref, value_ref,
):
    ylow, yhigh = edges(ynear_ref, yfar_ref, "xy")
    zlow, zhigh = edges(znear_ref, zfar_ref, "gz")

    def cell(y, z):
        if z == 0 or z == 5:
            return (zlow if z == 0 else zhigh)(y, 0)
        return ylow(0, z - 1) if y == 0 else (yhigh(0, z - 1) if y == 5 else f_ref[y - 1, z - 1])

    blends = blend(predictions(OUTER, cell, w_ref, bias_ref, heads_ref, hb_ref, g_ref))
    for i, (axis, at) in enumerate(OUTER_ROWS):
        value_ref[i : i + 1] = blends[at][axis : axis + 1]
    for axis in range(3):
        out_ref[axis * 16 : axis * 16 + 4] = value_ref[axis * 8 : axis * 8 + 4]
        out_ref[axis * 16 + 4 : axis * 16 + 12] = part_ref[axis * 8 : axis * 8 + 8]
        out_ref[axis * 16 + 12 : axis * 16 + 16] = value_ref[axis * 8 + 4 : axis * 8 + 8]
    both = counts_ref[...] + histogram(OUTER_ROWS, value_ref, col_ref, a_ref[:, 24 * 128 :], b_ref)
    table_ref[:256] = both[:, :128].astype(jnp.bfloat16)
    table_ref[256:] = both[:, 128:].astype(jnp.bfloat16)


def vmem(count):
    return [pl.BlockSpec(memory_space=pltpu.VMEM)] * count


def shape(dims, dtype):
    return jax.ShapeDtypeStruct(dims, dtype)


def in_hbm(array):
    return pltpu.with_memory_space_constraint(array, pltpu.HBM)


def arrange(*operands):
    yface, zface = shape((1, CORE, 64, 128), jnp.bfloat16), shape((CORE, 1, 64, 128), jnp.bfloat16)
    small = tuple(shape(o.shape, o.dtype) for o in operands[1:])
    return pl.pallas_call(
        arrange_kernel,
        out_shape=(shape((CORE, CORE, 64, 128), jnp.bfloat16), yface, yface, zface, zface) + small,
        in_specs=[pl.BlockSpec(memory_space=pltpu.HBM)] * (1 + SMALL),
        out_specs=tuple(vmem(5 + SMALL)),
        scratch_shapes=[
            pltpu.VMEM((1024, 128), jnp.float32), pltpu.VMEM((1024, 128), jnp.bfloat16),
            pltpu.SemaphoreType.DMA((4 + SMALL,)),
        ],
        compiler_params=pltpu.CompilerParams(vmem_limit_bytes=VMEM_LIMIT),
        name="arrange",
    )(*map(in_hbm, operands))


def prepare(taps, *operands):
    return pl.pallas_call(
        prepare_kernel,
        out_shape=(
            shape((192, 1024), jnp.bfloat16), shape((64, 128), jnp.float32), shape((8, 128), jnp.float32),
            shape((32, 256), jnp.bfloat16), shape((256, 6144), jnp.bfloat16), shape((48, 128), jnp.float32),
        ),
        in_specs=[pl.BlockSpec(memory_space=pltpu.HBM)] + vmem(6),
        out_specs=tuple(vmem(6)),
        scratch_shapes=[pltpu.VMEM((48, 128), jnp.float32), pltpu.VMEM(taps.shape, taps.dtype), pltpu.SemaphoreType.DMA(())],
        compiler_params=pltpu.CompilerParams(vmem_limit_bytes=VMEM_LIMIT),
        cost_estimate=pl.CostEstimate(flops=10**9, bytes_accessed=10**7, transcendentals=0),
        name="prepare",
    )(in_hbm(taps), *operands)


def inner(*operands):
    return pl.pallas_call(
        inner_kernel,
        out_shape=(shape((24, 128), jnp.float32), shape((256, 256), jnp.float32)),
        in_specs=vmem(9),
        out_specs=tuple(vmem(2)),
        scratch_shapes=[pltpu.VMEM((6 * 192, 512), jnp.bfloat16), pltpu.VMEM((256, 3072), jnp.bfloat16)],
        compiler_params=pltpu.CompilerParams(vmem_limit_bytes=VMEM_LIMIT),
        cost_estimate=pl.CostEstimate(flops=2 * 10**9, bytes_accessed=10**6, transcendentals=0),
        name="inner",
    )(*operands)


def outer(*operands):
    return pl.pallas_call(
        outer_kernel,
        out_shape=(shape((48, 128), jnp.float32), shape((512, 128), jnp.bfloat16)),
        in_specs=vmem(13),
        out_specs=tuple(vmem(2)),
        scratch_shapes=[
            pltpu.VMEM((6 * 192, 256), jnp.bfloat16), pltpu.VMEM((256, 3072), jnp.bfloat16),
            pltpu.VMEM((24, 128), jnp.float32),
        ],
        compiler_params=pltpu.CompilerParams(vmem_limit_bytes=VMEM_LIMIT),
        name="outer",
    )(*operands)


def finish_kernel(values_ref, sums_ref, out_ref, share_ref):
    out_ref[...] = values_ref[...]
    share_ref[...] = jnp.sum(sums_ref[...], axis=0, keepdims=True)


def finish(*operands):
    return pl.pallas_call(
        finish_kernel,
        out_shape=(shape((48, 128), jnp.float32), shape((1, 128), jnp.float32)),
        in_specs=vmem(2),
        out_specs=tuple(vmem(2)),
        compiler_params=pltpu.CompilerParams(vmem_limit_bytes=2 * 1024 * 1024),
        name="finish",
    )(*operands)


def groups(kept):
    axes = [axis for axis in FIELDS if axis not in kept] + list(kept)
    ids = np.arange(512).reshape(4, 8, 8, 2).transpose([list(FIELDS).index(axis) for axis in axes])
    return ids.reshape(-1, members(kept)).tolist()


def members(kept):
    return 2 ** sum(FIELDS[axis][1] for axis in kept)


def on_device(features, conv_w, conv_b, head_w, head_b, bins, edge_ids, owner_map):
    last = CORE - 1
    cells, ynear, yfar, znear, zfar, ids, bins, owner_map, conv_b, head_b, head_w = arrange(
        features.reshape(1024, 128), edge_ids.reshape(48, 128), bins.reshape(16, 128), owner_map.reshape(32, 128),
        conv_b.reshape(1, 64), head_b.reshape(1, 3), head_w,
    )
    ynear, yfar = swaps("xy", ynear, yfar)
    taps = jnp.transpose(conv_w, (2, 3, 4, 0, 1))
    weights, bias, offset, heads, owners, columns = prepare(taps, conv_b, head_b, head_w, ids, bins, owner_map)
    yeven, zeven = is_even("xy"), is_even("gz")
    ylow, yhigh = jnp.where(yeven, yfar, ynear), jnp.where(yeven, ynear, yfar)

    def with_corners(face, even):
        low = jnp.where(even, ylow[:, last:], ylow[:, :1])
        high = jnp.where(even, yhigh[:, last:], yhigh[:, :1])
        return jnp.concatenate([low, face, high], axis=0)

    znear, zfar = swaps("gz", with_corners(znear, zeven), with_corners(zfar, jnp.logical_not(zeven)))
    part, counts = inner(cells, yfar, ynear, weights, bias, heads, offset, owners, columns)
    blended, table = outer(
        cells, yfar, ynear, zfar, znear, weights, bias, heads, offset, owners, columns, part, counts
    )
    every = ("gz", "xy")
    one, two = EXCHANGES
    parts = table.reshape(members(one), members(two), 128)
    parts = lax.all_to_all(parts, every, 0, 0, tiled=True, axis_index_groups=groups(one))
    sums = jnp.sum(parts.astype(jnp.float32), axis=0)
    sums = lax.all_to_all(sums, every, 0, 0, tiled=True, axis_index_groups=groups(two))
    blended, share = finish(blended, sums)
    return blended.reshape(3, CORE, CORE, 128), share


def solution(mesh):
    in_specs = (
        P(None, "gz", "xy", None),
        P(),
        P(),
        P(),
        P(),
        P("gz", "xy", None),
        P(None, "gz", "xy", None),
        P(),
    )
    out_specs = (P(None, "gz", "xy", None), P(("gz", "xy"), None))
    return jax.shard_map(
        on_device, mesh=mesh, in_specs=in_specs, out_specs=out_specs, check_vma=False
    )
```

```python
import jax
import jax.numpy as jnp
import numpy as np
from jax import lax
from jax.experimental import pallas as pl
from jax.experimental.pallas import tpu as pltpu
from jax.sharding import PartitionSpec as P

BINS = 16
CORE = 4
TAPS = 3
SMALL = 5
FULL = (0, 1, 2)
VMEM_LIMIT = 32 * 1024 * 1024

VARIANTS = ((0, FULL), (1, FULL), (1, (0, 1)), (2, (1, 2)), (2, FULL), (3, FULL))
FIELDS = {"x": (7, 2), "y": (4, 3), "z": (1, 3), "c": (0, 1)}
EXCHANGES = ("xc", "yz")
INNER = (1, 2, 3, 4)
OUTER = (0, 5)
INNER_ROWS = [(axis, at) for axis in range(3) for at in range(4, 12)]
OUTER_ROWS = [(axis, at) for axis in range(3) for at in (0, 1, 2, 3, 12, 13, 14, 15)]


def swaps(axis, inside, outside):
    peers = lax.axis_size(axis)
    near = [(i, i ^ 1) for i in range(peers)]
    far = [(i, ((i + 1) ^ 1) - 1) for i in range(1, peers - 1)]
    return lax.ppermute(inside, axis, near), lax.ppermute(outside, axis, far)


def is_even(axis):
    return lax.axis_index(axis) % 2 == 0


def variant_weights(axis):
    index, total = lax.axis_index(axis), lax.axis_size(axis)
    lower = jnp.where(index > 0, 1.0, 0.0)
    upper = jnp.where(index < total - 1, 1.0, 0.0)
    weights = (3.0 + 2.0 * lower, 4.0, lower, upper, 4.0, 3.0 + 2.0 * upper)
    cover = (3.0 + 2.0 * lower, 4.0 + lower, 4.0 + upper, 3.0 + 2.0 * upper)
    return weights, cover


def column_of(row, size):
    length = row.shape[1]
    down = lax.broadcasted_iota(jnp.int32, (size, length), 0)
    along = lax.broadcasted_iota(jnp.int32, (size, length), 1)
    return jnp.broadcast_to(jnp.sum(jnp.where(down == along, row, 0.0), axis=1, keepdims=True), (size, 128))


def arrange_kernel(f_ref, *refs):
    sources, refs = refs[:SMALL], refs[SMALL:]
    (cells_ref, ynear_ref, yfar_ref, znear_ref, zfar_ref), refs = refs[:5], refs[5:]
    targets, (wide, f_v, sems) = refs[:SMALL], refs[SMALL:]
    parts = [slice(i * 256, i * 256 + 256) for i in range(4)]
    copies = [pltpu.make_async_copy(f_ref.at[part], f_v.at[part], sems.at[i]) for i, part in enumerate(parts)]
    copies += [pltpu.make_async_copy(src, dst, sems.at[4 + i]) for i, (src, dst) in enumerate(zip(sources, targets))]
    for copy in copies:
        copy.start()
    for i, part in enumerate(parts):
        copies[i].wait()
        wide[part] = f_v[part].astype(jnp.float32)
        for y in range(CORE):
            for z in range(CORE):
                piece = wide[pl.ds(i * 256 + z * CORE + y, 16, stride=16), :].astype(jnp.bfloat16)
                cells_ref[y, z, i * 16 : i * 16 + 16] = piece
    cells = cells_ref
    last = CORE - 1
    even = is_even("xy")
    for z in range(CORE):
        ynear_ref[0, z] = jnp.where(even, cells[last, z], cells[0, z])
        yfar_ref[0, z] = jnp.where(even, cells[0, z], cells[last, z])
    even = is_even("gz")
    for y in range(CORE):
        znear_ref[y, 0] = jnp.where(even, cells[y, last], cells[y, 0])
        zfar_ref[y, 0] = jnp.where(even, cells[y, 0], cells[y, last])
    for copy in copies[4:]:
        copy.wait()


def prepare_kernel(
    taps_hbm, cb_ref, hb_ref, ids_ref, bins_ref, map_ref, w_ref, bias_ref, off_ref, a_ref, col_ref,
    row_ref, taps_ref, sem,
):
    fetch = pltpu.make_async_copy(taps_hbm, taps_ref, sem)
    fetch.start()
    lookup(ids_ref, bins_ref, map_ref, a_ref, col_ref, row_ref)
    fetch.wait()
    for dx in range(TAPS):
        rows = jnp.concatenate([taps_ref[t % 3, t // 3, dx] for t in range(9)], axis=1)
        w_ref[64 * dx : 64 * dx + 64, :576] = rows
        w_ref[64 * dx : 64 * dx + 64, 640:1024] = rows[:, 192:]
    bias_ref[...] = column_of(cb_ref[...], 64)
    off_ref[...] = column_of(hb_ref[...], 8)


def lookup(ids_ref, bins_ref, map_ref, a_ref, col_ref, row_ref):
    one = jnp.ones((), jnp.bfloat16)
    none = jnp.zeros((), jnp.bfloat16)
    bins = bins_ref[...]
    for block in range(6):
        rows = slice(block * 8, block * 8 + 8)
        ids = ids_ref[rows]
        edge = jnp.maximum(ids, 0)
        low = edge & 127
        high = edge >> 7
        slot = jnp.zeros((8, 128), jnp.int32)
        for h in range(32):
            line = jnp.broadcast_to(map_ref[h : h + 1], (8, 128))
            slot = jnp.where(high == h, jnp.take_along_axis(line, low, axis=1, mode="promise_in_bounds"), slot)
        owner = slot >> 3
        place, shift = 0, 9
        for axis in "".join(EXCHANGES):
            low, width = FIELDS[axis]
            shift -= width
            place += ((owner >> low) & (2**width - 1)) << shift
        first = block % 2 * 8
        column = (place >> 8) * 128 + (slot & 7) * BINS + bins[first : first + 8]
        col_ref[rows] = jnp.where(ids >= 0, column, -1).astype(jnp.float32)
        row_ref[rows] = (place & 255).astype(jnp.float32)
    count = lax.broadcasted_iota(jnp.int32, (256, 128), 0).astype(jnp.float32).astype(jnp.bfloat16)
    for i, (axis, at) in enumerate(INNER_ROWS + OUTER_ROWS):
        r = axis * 16 + at
        row = row_ref[r : r + 1].astype(jnp.bfloat16)
        a_ref[:, i * 128 : i * 128 + 128] = jnp.where(count == row, one, none)


def predictions(zs, cell, w_ref, bias_ref, heads_ref, hb_ref, g_ref):
    width = 128 * len(zs)
    zero = jnp.zeros((64, 128), jnp.bfloat16)
    for y in range(6):
        for dz in range(TAPS):
            for i, v in enumerate(zs):
                z, kept = VARIANTS[v]
                part = cell(y, z + dz) if dz in kept else zero
                g_ref[(y * 3 + dz) * 64 : (y * 3 + dz) * 64 + 64, i * 128 : i * 128 + 128] = part
    lane = lax.broadcasted_iota(jnp.int32, (64, 128), 1)
    bias = bias_ref[...]
    preds = {}

    def matmul(left, right):
        return lax.dot_general(left, right, (((1,), (0,)), ((), ())), preferred_element_type=jnp.float32)

    def activate(p):
        hidden = []
        for half in range(2):
            q = p[:, half * 128 : half * 128 + 128]
            before = jnp.where(lane == 0, 0.0, pltpu.roll(q[:64], 1, 1))
            after = jnp.where(lane == 127, 0.0, pltpu.roll(q[128:], 127, 1))
            pre = before + q[64:128] + after
            hidden.append(jnp.maximum(pre + bias, 0.0).astype(jnp.bfloat16))
        return jnp.concatenate(hidden, axis=1)

    def head(batch):
        hidden = jnp.concatenate([h for _, _, h in batch], axis=0)
        rows = len(batch)
        logits = matmul(heads_ref[: 8 * rows, : 64 * rows], hidden)
        for i, (yv, start, _) in enumerate(batch):
            for half in range(2):
                logit = logits[i * 8 : i * 8 + 3, half * 128 : half * 128 + 128] + hb_ref[:3]
                preds[zs[start // 128 + half], yv] = jax.nn.sigmoid(logit)

    batch = []
    for start in range(0, width, 256):
        cols = slice(start, start + 256)

        def finish(yv, p):
            batch.append((yv, start, activate(p)))
            if len(batch) == 4:
                head(batch)
                batch.clear()

        finish(0, matmul(w_ref[:, :576], g_ref[:576, cols]))
        cut = matmul(w_ref[:, :384], g_ref[192:576, cols])
        finish(2, cut)
        finish(1, cut + matmul(w_ref[:, 832:1024], g_ref[576:768, cols]))
        cut = matmul(w_ref[:, 640:1024], g_ref[576:960, cols])
        finish(3, cut)
        finish(4, cut + matmul(w_ref[:, :192], g_ref[384:576, cols]))
        finish(5, matmul(w_ref[:, :576], g_ref[576:1152, cols]))
    if batch:
        head(batch)
    return preds


def blend(preds):
    zweights, zcover = variant_weights("gz")
    yweights, ycover = variant_weights("xy")
    totals = {}
    for (zv, yv), pred in preds.items():
        at = VARIANTS[zv][0] * CORE + VARIANTS[yv][0]
        term = pred * (zweights[zv] * yweights[yv])
        totals[at] = term if at not in totals else totals[at] + term
    return {at: total / (zcover[at // CORE] * ycover[at % CORE]) for at, total in totals.items()}


def histogram(rows, value_ref, col_ref, a_ref, b_ref):
    count = lax.broadcasted_iota(jnp.int32, (256, 128), 0).astype(jnp.float32).astype(jnp.bfloat16)
    none = jnp.zeros((), jnp.bfloat16)
    for i, (axis, at) in enumerate(rows):
        r = axis * 16 + at
        here = count == col_ref[r : r + 1].astype(jnp.bfloat16)
        b_ref[:, i * 128 : i * 128 + 128] = jnp.where(here, value_ref[i : i + 1].astype(jnp.bfloat16), none)
    return lax.dot_general(a_ref, b_ref[...], (((1,), (1,)), ((), ())), preferred_element_type=jnp.float32)


def edges(near_ref, far_ref, axis):
    even = is_even(axis)

    def low(*at):
        return jnp.where(even, far_ref[at], near_ref[at])

    def high(*at):
        return jnp.where(even, near_ref[at], far_ref[at])

    return low, high


def inner_kernel(
    f_ref, yfar_ref, ynear_ref, w_ref, bias_ref, hw_ref, hb_ref, a_ref, col_ref, part_ref, counts_ref, heads_ref, g_ref, b_ref
):
    head = jnp.concatenate([hw_ref[...].astype(jnp.float32), jnp.zeros((5, 64), jnp.float32)], axis=0)
    blank = jnp.zeros((8, 64), jnp.float32)
    lines = [jnp.concatenate([head if u == v else blank for u in range(4)], axis=1) for v in range(4)]
    heads_ref[...] = jnp.concatenate(lines, axis=0).astype(jnp.bfloat16)
    ylow, yhigh = edges(ynear_ref, yfar_ref, "xy")

    def cell(y, z):
        return ylow(0, z - 1) if y == 0 else (yhigh(0, z - 1) if y == 5 else f_ref[y - 1, z - 1])

    blends = blend(predictions(INNER, cell, w_ref, bias_ref, heads_ref, hb_ref, g_ref))
    for i, (axis, at) in enumerate(INNER_ROWS):
        part_ref[i : i + 1] = blends[at][axis : axis + 1]
    counts_ref[...] = histogram(INNER_ROWS, part_ref, col_ref, a_ref[:, : 24 * 128], b_ref)


def outer_kernel(
    f_ref, yfar_ref, ynear_ref, zfar_ref, znear_ref, w_ref, bias_ref, heads_ref, hb_ref, a_ref, col_ref, part_ref, counts_ref,
    out_ref, table_ref, g_ref, b_ref, value_ref,
):
    ylow, yhigh = edges(ynear_ref, yfar_ref, "xy")
    zlow, zhigh = edges(znear_ref, zfar_ref, "gz")

    def cell(y, z):
        if z == 0 or z == 5:
            return (zlow if z == 0 else zhigh)(y, 0)
        return ylow(0, z - 1) if y == 0 else (yhigh(0, z - 1) if y == 5 else f_ref[y - 1, z - 1])

    blends = blend(predictions(OUTER, cell, w_ref, bias_ref, heads_ref, hb_ref, g_ref))
    for i, (axis, at) in enumerate(OUTER_ROWS):
        value_ref[i : i + 1] = blends[at][axis : axis + 1]
    for axis in range(3):
        out_ref[axis * 16 : axis * 16 + 4] = value_ref[axis * 8 : axis * 8 + 4]
        out_ref[axis * 16 + 4 : axis * 16 + 12] = part_ref[axis * 8 : axis * 8 + 8]
        out_ref[axis * 16 + 12 : axis * 16 + 16] = value_ref[axis * 8 + 4 : axis * 8 + 8]
    both = counts_ref[...] + histogram(OUTER_ROWS, value_ref, col_ref, a_ref[:, 24 * 128 :], b_ref)
    table_ref[:256] = both[:, :128].astype(jnp.bfloat16)
    table_ref[256:] = both[:, 128:].astype(jnp.bfloat16)


def vmem(count):
    return [pl.BlockSpec(memory_space=pltpu.VMEM)] * count


def shape(dims, dtype):
    return jax.ShapeDtypeStruct(dims, dtype)


def in_hbm(array):
    return pltpu.with_memory_space_constraint(array, pltpu.HBM)


def arrange(*operands):
    yface, zface = shape((1, CORE, 64, 128), jnp.bfloat16), shape((CORE, 1, 64, 128), jnp.bfloat16)
    small = tuple(shape(o.shape, o.dtype) for o in operands[1:])
    return pl.pallas_call(
        arrange_kernel,
        out_shape=(shape((CORE, CORE, 64, 128), jnp.bfloat16), yface, yface, zface, zface) + small,
        in_specs=[pl.BlockSpec(memory_space=pltpu.HBM)] * (1 + SMALL),
        out_specs=tuple(vmem(5 + SMALL)),
        scratch_shapes=[
            pltpu.VMEM((1024, 128), jnp.float32), pltpu.VMEM((1024, 128), jnp.bfloat16),
            pltpu.SemaphoreType.DMA((4 + SMALL,)),
        ],
        compiler_params=pltpu.CompilerParams(vmem_limit_bytes=VMEM_LIMIT),
        name="arrange",
    )(*map(in_hbm, operands))


def prepare(taps, *operands):
    return pl.pallas_call(
        prepare_kernel,
        out_shape=(
            shape((192, 1024), jnp.bfloat16), shape((64, 128), jnp.float32), shape((8, 128), jnp.float32),
            shape((256, 6144), jnp.bfloat16), shape((48, 128), jnp.float32),
        ),
        in_specs=[pl.BlockSpec(memory_space=pltpu.HBM)] + vmem(5),
        out_specs=tuple(vmem(5)),
        scratch_shapes=[pltpu.VMEM((48, 128), jnp.float32), pltpu.VMEM(taps.shape, taps.dtype), pltpu.SemaphoreType.DMA(())],
        compiler_params=pltpu.CompilerParams(vmem_limit_bytes=VMEM_LIMIT),
        cost_estimate=pl.CostEstimate(flops=10**9, bytes_accessed=10**7, transcendentals=0),
        name="prepare",
    )(in_hbm(taps), *operands)


def inner(*operands):
    return pl.pallas_call(
        inner_kernel,
        out_shape=(shape((24, 128), jnp.float32), shape((256, 256), jnp.float32), shape((32, 256), jnp.bfloat16)),
        in_specs=vmem(9),
        out_specs=tuple(vmem(3)),
        scratch_shapes=[pltpu.VMEM((6 * 192, 512), jnp.bfloat16), pltpu.VMEM((256, 3072), jnp.bfloat16)],
        compiler_params=pltpu.CompilerParams(vmem_limit_bytes=VMEM_LIMIT),
        cost_estimate=pl.CostEstimate(flops=2 * 10**9, bytes_accessed=10**6, transcendentals=0),
        name="inner",
    )(*operands)


def outer(*operands):
    return pl.pallas_call(
        outer_kernel,
        out_shape=(shape((48, 128), jnp.float32), shape((512, 128), jnp.bfloat16)),
        in_specs=vmem(13),
        out_specs=tuple(vmem(2)),
        scratch_shapes=[
            pltpu.VMEM((6 * 192, 256), jnp.bfloat16), pltpu.VMEM((256, 3072), jnp.bfloat16),
            pltpu.VMEM((24, 128), jnp.float32),
        ],
        compiler_params=pltpu.CompilerParams(vmem_limit_bytes=VMEM_LIMIT),
        name="outer",
    )(*operands)


def finish_kernel(values_ref, sums_ref, out_ref, share_ref):
    out_ref[...] = values_ref[...]
    share_ref[...] = jnp.sum(sums_ref[...], axis=0, keepdims=True)


def finish(*operands):
    return pl.pallas_call(
        finish_kernel,
        out_shape=(shape((48, 128), jnp.float32), shape((1, 128), jnp.float32)),
        in_specs=vmem(2),
        out_specs=tuple(vmem(2)),
        compiler_params=pltpu.CompilerParams(vmem_limit_bytes=2 * 1024 * 1024),
        name="finish",
    )(*operands)


def groups(kept):
    axes = [axis for axis in FIELDS if axis not in kept] + list(kept)
    ids = np.arange(512).reshape(4, 8, 8, 2).transpose([list(FIELDS).index(axis) for axis in axes])
    return ids.reshape(-1, members(kept)).tolist()


def members(kept):
    return 2 ** sum(FIELDS[axis][1] for axis in kept)


def on_device(features, conv_w, conv_b, head_w, head_b, bins, edge_ids, owner_map):
    last = CORE - 1
    cells, ynear, yfar, znear, zfar, ids, bins, owner_map, conv_b, head_b = arrange(
        features.reshape(1024, 128), edge_ids.reshape(48, 128), bins.reshape(16, 128), owner_map.reshape(32, 128),
        conv_b.reshape(1, 64), head_b.reshape(1, 3),
    )
    ynear, yfar = swaps("xy", ynear, yfar)
    taps = jnp.transpose(conv_w, (2, 3, 4, 0, 1))
    weights, bias, offset, owners, columns = prepare(taps, conv_b, head_b, ids, bins, owner_map)
    yeven, zeven = is_even("xy"), is_even("gz")
    ylow, yhigh = jnp.where(yeven, yfar, ynear), jnp.where(yeven, ynear, yfar)

    def with_corners(face, even):
        low = jnp.where(even, ylow[:, last:], ylow[:, :1])
        high = jnp.where(even, yhigh[:, last:], yhigh[:, :1])
        return jnp.concatenate([low, face, high], axis=0)

    znear, zfar = swaps("gz", with_corners(znear, zeven), with_corners(zfar, jnp.logical_not(zeven)))
    part, counts, heads = inner(cells, yfar, ynear, weights, bias, head_w, offset, owners, columns)
    blended, table = outer(
        cells, yfar, ynear, zfar, znear, weights, bias, heads, offset, owners, columns, part, counts
    )
    every = ("gz", "xy")
    one, two = EXCHANGES
    parts = table.reshape(members(one), members(two), 128)
    parts = lax.all_to_all(parts, every, 0, 0, tiled=True, axis_index_groups=groups(one))
    sums = jnp.sum(parts.astype(jnp.float32), axis=0)
    sums = lax.all_to_all(sums, every, 0, 0, tiled=True, axis_index_groups=groups(two))
    blended, share = finish(blended, sums)
    return blended.reshape(3, CORE, CORE, 128), share


def solution(mesh):
    in_specs = (
        P(None, "gz", "xy", None),
        P(),
        P(),
        P(),
        P(),
        P("gz", "xy", None),
        P(None, "gz", "xy", None),
        P(),
    )
    out_specs = (P(None, "gz", "xy", None), P(("gz", "xy"), None))
    return jax.shard_map(
        on_device, mesh=mesh, in_specs=in_specs, out_specs=out_specs, check_vma=False
    )
```

```python
import jax
import jax.numpy as jnp
import numpy as np
from jax import lax
from jax.experimental import pallas as pl
from jax.experimental.pallas import tpu as pltpu
from jax.sharding import PartitionSpec as P

BINS = 16
CORE = 4
TAPS = 3
SMALL = 5
FULL = (0, 1, 2)
VMEM_LIMIT = 32 * 1024 * 1024

VARIANTS = ((0, FULL), (1, FULL), (1, (0, 1)), (2, (1, 2)), (2, FULL), (3, FULL))
FIELDS = {"x": (7, 2), "y": (4, 3), "z": (1, 3), "c": (0, 1)}
EXCHANGES = ("xc", "yz")
INNER = (1, 2, 3, 4)
OUTER = (0, 5)
INNER_ROWS = [(axis, at) for axis in range(3) for at in range(4, 12)]
OUTER_ROWS = [(axis, at) for axis in range(3) for at in (0, 1, 2, 3, 12, 13, 14, 15)]


def swaps(axis, inside, outside):
    peers = lax.axis_size(axis)
    near = [(i, i ^ 1) for i in range(peers)]
    far = [(i, ((i + 1) ^ 1) - 1) for i in range(1, peers - 1)]
    return lax.ppermute(inside, axis, near), lax.ppermute(outside, axis, far)


def is_even(axis):
    return lax.axis_index(axis) % 2 == 0


def variant_weights(axis):
    index, total = lax.axis_index(axis), lax.axis_size(axis)
    lower = jnp.where(index > 0, 1.0, 0.0)
    upper = jnp.where(index < total - 1, 1.0, 0.0)
    weights = (3.0 + 2.0 * lower, 4.0, lower, upper, 4.0, 3.0 + 2.0 * upper)
    cover = (3.0 + 2.0 * lower, 4.0 + lower, 4.0 + upper, 3.0 + 2.0 * upper)
    return weights, cover


def column_of(row, size):
    length = row.shape[1]
    down = lax.broadcasted_iota(jnp.int32, (size, length), 0)
    along = lax.broadcasted_iota(jnp.int32, (size, length), 1)
    return jnp.broadcast_to(jnp.sum(jnp.where(down == along, row, 0.0), axis=1, keepdims=True), (size, 128))


def arrange_kernel(f_ref, *refs):
    sources, refs = refs[:SMALL], refs[SMALL:]
    (cells_ref, ynear_ref, yfar_ref, znear_ref, zfar_ref), refs = refs[:5], refs[5:]
    targets, (wide, f_v, sems) = refs[:SMALL], refs[SMALL:]
    parts = [slice(i * 256, i * 256 + 256) for i in range(4)]
    copies = [pltpu.make_async_copy(f_ref.at[part], f_v.at[part], sems.at[i]) for i, part in enumerate(parts)]
    copies += [pltpu.make_async_copy(src, dst, sems.at[4 + i]) for i, (src, dst) in enumerate(zip(sources, targets))]
    for copy in copies:
        copy.start()
    for i, part in enumerate(parts):
        copies[i].wait()
        wide[part] = f_v[part].astype(jnp.float32)
        for y in range(CORE):
            for z in range(CORE):
                piece = wide[pl.ds(i * 256 + z * CORE + y, 16, stride=16), :].astype(jnp.bfloat16)
                cells_ref[y, z, i * 16 : i * 16 + 16] = piece
    cells = cells_ref
    last = CORE - 1
    even = is_even("xy")
    for z in range(CORE):
        ynear_ref[0, z] = jnp.where(even, cells[last, z], cells[0, z])
        yfar_ref[0, z] = jnp.where(even, cells[0, z], cells[last, z])
    even = is_even("gz")
    for y in range(CORE):
        znear_ref[y, 0] = jnp.where(even, cells[y, last], cells[y, 0])
        zfar_ref[y, 0] = jnp.where(even, cells[y, 0], cells[y, last])
    for copy in copies[4:]:
        copy.wait()


def prepare_kernel(
    taps_hbm, cb_ref, hb_ref, ids_ref, bins_ref, map_ref, w_ref, bias_ref, off_ref, a_ref, col_ref, edge_ref,
    row_ref, taps_ref, sem,
):
    fetch = pltpu.make_async_copy(taps_hbm, taps_ref, sem)
    fetch.start()
    lookup(ids_ref, bins_ref, map_ref, a_ref, col_ref, row_ref)
    fetch.wait()
    for dx in range(TAPS):
        rows = jnp.concatenate([taps_ref[t % 3, t // 3, dx] for t in range(9)], axis=1)
        w_ref[64 * dx : 64 * dx + 64, :576] = rows
        w_ref[64 * dx : 64 * dx + 64, 640:1024] = rows[:, 192:]
        edge_ref[64 * dx : 64 * dx + 64] = jnp.concatenate([taps_ref[t % 2 * 2, t // 2, dx] for t in range(6)], axis=1)
    bias_ref[...] = column_of(cb_ref[...], 64)
    off_ref[...] = column_of(hb_ref[...], 8)


def lookup(ids_ref, bins_ref, map_ref, a_ref, col_ref, row_ref):
    one = jnp.ones((), jnp.bfloat16)
    none = jnp.zeros((), jnp.bfloat16)
    bins = bins_ref[...]
    for block in range(6):
        rows = slice(block * 8, block * 8 + 8)
        ids = ids_ref[rows]
        edge = jnp.maximum(ids, 0)
        low = edge & 127
        high = edge >> 7
        slot = jnp.zeros((8, 128), jnp.int32)
        for h in range(32):
            line = jnp.broadcast_to(map_ref[h : h + 1], (8, 128))
            slot = jnp.where(high == h, jnp.take_along_axis(line, low, axis=1, mode="promise_in_bounds"), slot)
        owner = slot >> 3
        place, shift = 0, 9
        for axis in "".join(EXCHANGES):
            low, width = FIELDS[axis]
            shift -= width
            place += ((owner >> low) & (2**width - 1)) << shift
        first = block % 2 * 8
        column = (place >> 8) * 128 + (slot & 7) * BINS + bins[first : first + 8]
        col_ref[rows] = jnp.where(ids >= 0, column, -1).astype(jnp.float32)
        row_ref[rows] = (place & 255).astype(jnp.float32)
    count = lax.broadcasted_iota(jnp.int32, (256, 128), 0).astype(jnp.float32).astype(jnp.bfloat16)
    for i, (axis, at) in enumerate(INNER_ROWS + OUTER_ROWS):
        r = axis * 16 + at
        row = row_ref[r : r + 1].astype(jnp.bfloat16)
        a_ref[:, i * 128 : i * 128 + 128] = jnp.where(count == row, one, none)


def matmul(left, right):
    return lax.dot_general(left, right, (((1,), (0,)), ((), ())), preferred_element_type=jnp.float32)


def convolve(weight, rows):
    yield 0, matmul(weight(0, 3), rows(0, 3))
    cut = matmul(weight(0, 2), rows(1, 3))
    yield 2, cut
    yield 1, cut + matmul(weight(2, 3), rows(3, 4))
    cut = matmul(weight(1, 3), rows(3, 5))
    yield 3, cut
    yield 4, cut + matmul(weight(0, 1), rows(2, 3))
    yield 5, matmul(weight(0, 3), rows(3, 6))


def whole(w_ref):
    return lambda first, end: w_ref[:, first * 192 : end * 192] if first == 0 else w_ref[:, 448 + first * 192 : 448 + end * 192]


def lay(zs, cell, g_ref, taps):
    zero = jnp.zeros((64, 128), jnp.bfloat16)
    for y in range(6):
        for at, dz in enumerate(taps):
            for i, v in enumerate(zs):
                z, kept = VARIANTS[v]
                part = cell(y, z + dz) if dz in kept else None
                first = (y * len(taps) + at) * 64
                g_ref[first : first + 64, i * 128 : i * 128 + 128] = zero if part is None else part


def predictions(zs, tiles, bias_ref, heads_ref, hb_ref):
    lane = lax.broadcasted_iota(jnp.int32, (64, 128), 1)
    bias = bias_ref[...]
    preds = {}

    def activate(p):
        hidden = []
        for half in range(2):
            q = p[:, half * 128 : half * 128 + 128]
            before = jnp.where(lane == 0, 0.0, pltpu.roll(q[:64], 1, 1))
            after = jnp.where(lane == 127, 0.0, pltpu.roll(q[128:], 127, 1))
            pre = before + q[64:128] + after
            hidden.append(jnp.maximum(pre + bias, 0.0).astype(jnp.bfloat16))
        return jnp.concatenate(hidden, axis=1)

    def head(batch):
        hidden = jnp.concatenate([h for _, _, h in batch], axis=0)
        rows = len(batch)
        logits = matmul(heads_ref[: 8 * rows, : 64 * rows], hidden)
        for i, (yv, start, _) in enumerate(batch):
            for half in range(2):
                logit = logits[i * 8 : i * 8 + 3, half * 128 : half * 128 + 128] + hb_ref[:3]
                preds[zs[start // 128 + half], yv] = jax.nn.sigmoid(logit)

    batch = []
    for tile, sums in enumerate(tiles):
        for yv, p in sums:
            batch.append((yv, tile * 256, activate(p)))
            if len(batch) == 4:
                head(batch)
                batch.clear()
    if batch:
        head(batch)
    return preds


def blend(preds):
    zweights, zcover = variant_weights("gz")
    yweights, ycover = variant_weights("xy")
    totals = {}
    for (zv, yv), pred in preds.items():
        at = VARIANTS[zv][0] * CORE + VARIANTS[yv][0]
        term = pred * (zweights[zv] * yweights[yv])
        totals[at] = term if at not in totals else totals[at] + term
    return {at: total / (zcover[at // CORE] * ycover[at % CORE]) for at, total in totals.items()}


def histogram(rows, value_ref, col_ref, a_ref, b_ref):
    count = lax.broadcasted_iota(jnp.int32, (256, 128), 0).astype(jnp.float32).astype(jnp.bfloat16)
    none = jnp.zeros((), jnp.bfloat16)
    for i, (axis, at) in enumerate(rows):
        r = axis * 16 + at
        here = count == col_ref[r : r + 1].astype(jnp.bfloat16)
        b_ref[:, i * 128 : i * 128 + 128] = jnp.where(here, value_ref[i : i + 1].astype(jnp.bfloat16), none)
    return lax.dot_general(a_ref, b_ref[...], (((1,), (1,)), ((), ())), preferred_element_type=jnp.float32)


def edges(near_ref, far_ref, axis):
    even = is_even(axis)

    def low(*at):
        return jnp.where(even, far_ref[at], near_ref[at])

    def high(*at):
        return jnp.where(even, near_ref[at], far_ref[at])

    return low, high


def inner_kernel(
    f_ref, yfar_ref, ynear_ref, w_ref, bias_ref, hw_ref, hb_ref, a_ref, col_ref, part_ref, counts_ref, heads_ref, own_ref,
    g_ref, b_ref, h_ref,
):
    head = jnp.concatenate([hw_ref[...].astype(jnp.float32), jnp.zeros((5, 64), jnp.float32)], axis=0)
    blank = jnp.zeros((8, 64), jnp.float32)
    lines = [jnp.concatenate([head if u == v else blank for u in range(4)], axis=1) for v in range(4)]
    heads_ref[...] = jnp.concatenate(lines, axis=0).astype(jnp.bfloat16)
    ylow, yhigh = edges(ynear_ref, yfar_ref, "xy")

    def cell(y, z):
        return ylow(0, z - 1) if y == 0 else (yhigh(0, z - 1) if y == 5 else f_ref[y - 1, z - 1])

    def own(y, z):
        return None if z in (0, 5) else cell(y, z)

    lay(INNER, cell, g_ref, FULL)
    tiles = [
        convolve(whole(w_ref), lambda first, end, at=at: g_ref[first * 192 : end * 192, at : at + 256]) for at in (0, 256)
    ]
    blends = blend(predictions(INNER, tiles, bias_ref, heads_ref, hb_ref))
    lay(OUTER, own, h_ref, FULL)
    for yv, p in convolve(whole(w_ref), lambda first, end: h_ref[first * 192 : end * 192]):
        own_ref[yv] = p
    for i, (axis, at) in enumerate(INNER_ROWS):
        part_ref[i : i + 1] = blends[at][axis : axis + 1]
    counts_ref[...] = histogram(INNER_ROWS, part_ref, col_ref, a_ref[:, : 24 * 128], b_ref)


def outer_kernel(
    znear_ref, zfar_ref, w_ref, bias_ref, heads_ref, hb_ref, a_ref, col_ref, part_ref, counts_ref, own_ref,
    out_ref, table_ref, g_ref, b_ref, value_ref,
):
    zlow, zhigh = edges(znear_ref, zfar_ref, "gz")

    def halo(y, z):
        return zlow(y, 0) if z == 0 else (zhigh(y, 0) if z == 5 else None)

    lay(OUTER, halo, g_ref, (0, 2))
    sums = convolve(
        lambda first, end: w_ref[:, first * 128 : end * 128], lambda first, end: g_ref[first * 128 : end * 128]
    )
    tiles = [((yv, p + own_ref[yv]) for yv, p in sums)]
    blends = blend(predictions(OUTER, tiles, bias_ref, heads_ref, hb_ref))
    for i, (axis, at) in enumerate(OUTER_ROWS):
        value_ref[i : i + 1] = blends[at][axis : axis + 1]
    for axis in range(3):
        out_ref[axis * 16 : axis * 16 + 4] = value_ref[axis * 8 : axis * 8 + 4]
        out_ref[axis * 16 + 4 : axis * 16 + 12] = part_ref[axis * 8 : axis * 8 + 8]
        out_ref[axis * 16 + 12 : axis * 16 + 16] = value_ref[axis * 8 + 4 : axis * 8 + 8]
    both = counts_ref[...] + histogram(OUTER_ROWS, value_ref, col_ref, a_ref[:, 24 * 128 :], b_ref)
    table_ref[:256] = both[:, :128].astype(jnp.bfloat16)
    table_ref[256:] = both[:, 128:].astype(jnp.bfloat16)


def vmem(count):
    return [pl.BlockSpec(memory_space=pltpu.VMEM)] * count


def shape(dims, dtype):
    return jax.ShapeDtypeStruct(dims, dtype)


def in_hbm(array):
    return pltpu.with_memory_space_constraint(array, pltpu.HBM)


def arrange(*operands):
    yface, zface = shape((1, CORE, 64, 128), jnp.bfloat16), shape((CORE, 1, 64, 128), jnp.bfloat16)
    small = tuple(shape(o.shape, o.dtype) for o in operands[1:])
    return pl.pallas_call(
        arrange_kernel,
        out_shape=(shape((CORE, CORE, 64, 128), jnp.bfloat16), yface, yface, zface, zface) + small,
        in_specs=[pl.BlockSpec(memory_space=pltpu.HBM)] * (1 + SMALL),
        out_specs=tuple(vmem(5 + SMALL)),
        scratch_shapes=[
            pltpu.VMEM((1024, 128), jnp.float32), pltpu.VMEM((1024, 128), jnp.bfloat16),
            pltpu.SemaphoreType.DMA((4 + SMALL,)),
        ],
        compiler_params=pltpu.CompilerParams(vmem_limit_bytes=VMEM_LIMIT),
        name="arrange",
    )(*map(in_hbm, operands))


def prepare(taps, *operands):
    return pl.pallas_call(
        prepare_kernel,
        out_shape=(
            shape((192, 1024), jnp.bfloat16), shape((64, 128), jnp.float32), shape((8, 128), jnp.float32),
            shape((256, 6144), jnp.bfloat16), shape((48, 128), jnp.float32), shape((192, 384), jnp.bfloat16),
        ),
        in_specs=[pl.BlockSpec(memory_space=pltpu.HBM)] + vmem(5),
        out_specs=tuple(vmem(6)),
        scratch_shapes=[pltpu.VMEM((48, 128), jnp.float32), pltpu.VMEM(taps.shape, taps.dtype), pltpu.SemaphoreType.DMA(())],
        compiler_params=pltpu.CompilerParams(vmem_limit_bytes=VMEM_LIMIT),
        cost_estimate=pl.CostEstimate(flops=10**9, bytes_accessed=10**7, transcendentals=0),
        name="prepare",
    )(in_hbm(taps), *operands)


def inner(*operands):
    return pl.pallas_call(
        inner_kernel,
        out_shape=(shape((24, 128), jnp.float32), shape((256, 256), jnp.float32), shape((32, 256), jnp.bfloat16), shape((6, 192, 256), jnp.float32)),
        in_specs=vmem(9),
        out_specs=tuple(vmem(4)),
        scratch_shapes=[pltpu.VMEM((6 * 192, 512), jnp.bfloat16), pltpu.VMEM((256, 3072), jnp.bfloat16), pltpu.VMEM((6 * 192, 256), jnp.bfloat16)],
        compiler_params=pltpu.CompilerParams(vmem_limit_bytes=VMEM_LIMIT),
        cost_estimate=pl.CostEstimate(flops=2 * 10**9, bytes_accessed=10**6, transcendentals=0),
        name="inner",
    )(*operands)


def outer(*operands):
    return pl.pallas_call(
        outer_kernel,
        out_shape=(shape((48, 128), jnp.float32), shape((512, 128), jnp.bfloat16)),
        in_specs=vmem(11),
        out_specs=tuple(vmem(2)),
        scratch_shapes=[
            pltpu.VMEM((6 * 128, 256), jnp.bfloat16), pltpu.VMEM((256, 3072), jnp.bfloat16),
            pltpu.VMEM((24, 128), jnp.float32),
        ],
        compiler_params=pltpu.CompilerParams(vmem_limit_bytes=VMEM_LIMIT),
        name="outer",
    )(*operands)


def finish_kernel(values_ref, sums_ref, out_ref, share_ref):
    out_ref[...] = values_ref[...]
    share_ref[...] = jnp.sum(sums_ref[...], axis=0, keepdims=True)


def finish(*operands):
    return pl.pallas_call(
        finish_kernel,
        out_shape=(shape((48, 128), jnp.float32), shape((1, 128), jnp.float32)),
        in_specs=vmem(2),
        out_specs=tuple(vmem(2)),
        compiler_params=pltpu.CompilerParams(vmem_limit_bytes=2 * 1024 * 1024),
        name="finish",
    )(*operands)


def groups(kept):
    axes = [axis for axis in FIELDS if axis not in kept] + list(kept)
    ids = np.arange(512).reshape(4, 8, 8, 2).transpose([list(FIELDS).index(axis) for axis in axes])
    return ids.reshape(-1, members(kept)).tolist()


def members(kept):
    return 2 ** sum(FIELDS[axis][1] for axis in kept)


def on_device(features, conv_w, conv_b, head_w, head_b, bins, edge_ids, owner_map):
    last = CORE - 1
    cells, ynear, yfar, znear, zfar, ids, bins, owner_map, conv_b, head_b = arrange(
        features.reshape(1024, 128), edge_ids.reshape(48, 128), bins.reshape(16, 128), owner_map.reshape(32, 128),
        conv_b.reshape(1, 64), head_b.reshape(1, 3),
    )
    ynear, yfar = swaps("xy", ynear, yfar)
    taps = jnp.transpose(conv_w, (2, 3, 4, 0, 1))
    weights, bias, offset, owners, columns, halo_weights = prepare(taps, conv_b, head_b, ids, bins, owner_map)
    yeven, zeven = is_even("xy"), is_even("gz")
    ylow, yhigh = jnp.where(yeven, yfar, ynear), jnp.where(yeven, ynear, yfar)

    def with_corners(face, even):
        low = jnp.where(even, ylow[:, last:], ylow[:, :1])
        high = jnp.where(even, yhigh[:, last:], yhigh[:, :1])
        return jnp.concatenate([low, face, high], axis=0)

    znear, zfar = swaps("gz", with_corners(znear, zeven), with_corners(zfar, jnp.logical_not(zeven)))
    part, counts, heads, own = inner(cells, yfar, ynear, weights, bias, head_w, offset, owners, columns)
    blended, table = outer(
        znear, zfar, halo_weights, bias, heads, offset, owners, columns, part, counts, own
    )
    every = ("gz", "xy")
    one, two = EXCHANGES
    parts = table.reshape(members(one), members(two), 128)
    parts = lax.all_to_all(parts, every, 0, 0, tiled=True, axis_index_groups=groups(one))
    sums = jnp.sum(parts.astype(jnp.float32), axis=0)
    sums = lax.all_to_all(sums, every, 0, 0, tiled=True, axis_index_groups=groups(two))
    blended, share = finish(blended, sums)
    return blended.reshape(3, CORE, CORE, 128), share


def solution(mesh):
    in_specs = (
        P(None, "gz", "xy", None),
        P(),
        P(),
        P(),
        P(),
        P("gz", "xy", None),
        P(None, "gz", "xy", None),
        P(),
    )
    out_specs = (P(None, "gz", "xy", None), P(("gz", "xy"), None))
    return jax.shard_map(
        on_device, mesh=mesh, in_specs=in_specs, out_specs=out_specs, check_vma=False
    )
```
